32 devices in a mesh: batch: 16 (over z, y, core), coef: 2 (over x).
Axes of the slice: x: 2, y: 2, z: 4, core: 2. Of those that a mesh axis runs over, the one named last changes fastest.
Arguments:
- jac_blocks: bfloat16 [128, 2, 2, 128, 128], P(('batch', 'coef')), may hold values from -0.52734375 to 0.52734375
- col_blocks: int32 [2, 128, 2], P('coef', 'batch'), may hold values from 0 to 15, all different within a row; in each aligned block of 8 rows (0 to 7, 8 to 15, ..., all dimensions but the last counted through in order) at most 2 rows name the same one
- residual: float32 [128, 128], P('batch'), may hold values from -6 to 6
- run_of_half: int32 [256], P('batch'), may hold values from 0 to 255, each once
- run_scale: bfloat16 [256], replicated, may hold values from 0.25 to 4
Outputs:
- diag_blocks: float32 [2, 16, 128, 128], P('coef', 'batch')
- gradient: float32 [2, 16, 128], P('coef', 'batch')
The draws below stay inside these ranges and needn't reach their ends.
Inputs may be any that keep to these rules, and one draw needn't show every extreme that they name: `col_blocks`: the 2 column blocks of one row block in one group differ. For each group, among the row blocks of one batch index (aligned blocks of the row-block dimension), no column block is named more than 2 times, a bound that some block reaches. `run_of_half`: every run appears exactly once.
All inputs are finite; a program needn't handle non-finite values.
Results may differ from the reference program's by a relative error of at most 0.00043.
Values may be sent and summed in bfloat16 or wider, within the bound.
A program may use at most 64 MiB of HBM per device.

```python
import math
import jax
import jax.numpy as jnp
import numpy as np
from jax import lax

BS = 128
PAIR = 2
CAP = 2
R_DEV = 4
G = 2
LCB = 16
NRB = 128
RUNS = 256
N_COEF = 2


def steps_of(own_key, dims, cuts, low, largest):
    factor_of, own = 1.0, jax.random.fold_in(own_key, 6)
    for position, blocks in cuts:
        steps = jnp.exp(jax.random.uniform(jax.random.fold_in(own, position), (blocks,), jnp.float32, low / len(cuts), largest / len(cuts)))
        factor_of = factor_of * jnp.repeat(steps, dims[position] // blocks).reshape([-1 if axis == position else 1 for axis in range(len(dims))])
    return factor_of


def assign_block(key, own, number, rows, count, top, limit, slope):
    order = jax.random.permutation(key, count)
    packed, common = portions_of(count, rows * top, limit, slope, True), portions_of(count, rows * top, limit, slope, False)
    places = jnp.arange(count)

    def named(tallies, offset_by):
        used = int((tallies > 0).sum())
        fixed = max(1, used // 4)
        moved = fixed + (places - fixed + offset_by * (used - fixed)) % max(1, count - fixed)
        return jnp.zeros((count,), jnp.int32).at[order[jnp.where(places < fixed, places, moved)]].set(jnp.asarray(tallies, jnp.int32))

    tallies = jnp.where(number % 4 == 0, named(packed, number // 4), named(common, number - number // 4 - 1))
    mixed = jax.random.permutation(jax.random.fold_in(own, 3), count)
    donor, receiver = mixed[0:count // 2 * 2:2], mixed[1:count // 2 * 2:2]
    margin = jnp.minimum(tallies[donor] - 1, limit - tallies[receiver]) // 2
    margin = jnp.where((donor == order[0]) | (receiver == order[0]) | (tallies[receiver] == 0), 0, jnp.maximum(margin, 0))
    moved = jax.random.randint(jax.random.fold_in(own, 4), (count // 2,), 0, 1 << 20) % (margin + 1)
    tallies = tallies.at[donor].add(-moved).at[receiver].add(moved)
    members = jnp.searchsorted(jnp.cumsum(tallies), jnp.arange(rows * top), side="right").astype(jnp.int32)
    table = members.reshape(top, rows).T
    table = table[jax.random.permutation(jax.random.fold_in(own, 1), rows)]
    offset_by = jax.random.randint(jax.random.fold_in(own, 2), (rows, 1), 0, top)
    return jnp.take_along_axis(table, (jnp.arange(top)[None, :] + offset_by) % top, axis=1)


def portions_of(number_of, total, bound, skew, full):
    loads = [(1 << 20) // math.isqrt(standing ** skew) + 1 for standing in range(1, number_of + 1)]
    largest = bound if full else min(bound, max(-(-total // number_of), total * loads[0] // sum(loads)))
    least = 1 if total - largest >= number_of - 1 else 0
    given, rest = [largest] + [least] * (number_of - 1), total - largest - least * (number_of - 1)
    while rest > 0:
        movable = [i for i in range(1, number_of) if given[i] < largest] or [i for i in range(1, number_of) if given[i] < bound]
        mass, left = sum([loads[i] for i in movable]), rest
        for i in movable:
            more = min(bound - given[i], max(1, left * loads[i] // mass), rest)
            given[i] = given[i] + more
            rest = rest - more
    return np.array(given)


def noise(own_key, shape, width, reach, cuts=(), kind=jnp.bfloat16):
    result = jax.random.normal(own_key, shape, jnp.float32) * width
    if len(cuts) > 0:
        result = steps_of(own_key, shape, cuts, -0.22, 0.18) * result
    return jnp.clip(result, min=-reach, max=reach).astype(kind)


def setup_inputs(seed: int = 0) -> dict:
    splits = jax.random.split(jax.random.key(seed), 6)
    jac_blocks = noise(splits[0], (NRB, G, PAIR, BS, BS), (1.0 / BS ** 0.5), 0.52734375, ((0, 32),))
    col_blocks_keys = jax.random.split(jax.random.fold_in(splits[1], 1), G * NRB // (R_DEV * N_COEF))
    col_blocks_turns = jax.random.permutation(jax.random.fold_in(splits[1], 3), G * NRB // (R_DEV * N_COEF))
    col_blocks = jax.vmap(lambda own, number: assign_block(jax.random.fold_in(splits[1], 2), own, number, R_DEV * N_COEF, LCB, PAIR, CAP, 2))(col_blocks_keys, col_blocks_turns).reshape((G, NRB, PAIR))
    residual = noise(splits[2], (NRB, BS), 1.0, 6.0, ((0, 16),), jnp.float32)
    run_of_half = jax.random.permutation(splits[3], RUNS).astype(jnp.int32)
    run_scale = jnp.clip(jnp.exp(jax.random.uniform(splits[4], (RUNS,), jnp.float32, math.log(0.25), math.log(4.0))), 0.25, 4.0).astype(jnp.bfloat16)
    return dict(jac_blocks=jac_blocks, col_blocks=col_blocks, residual=residual, run_of_half=run_of_half, run_scale=run_scale)


def reference(jac_blocks, col_blocks, residual, run_of_half, run_scale):
    scale_rows = run_scale.astype(jnp.float32)[run_of_half].reshape(NRB, 2)
    weights = jnp.repeat(scale_rows, BS // 2, axis=1)
    cols_by_row = jnp.transpose(col_blocks, (1, 0, 2)).astype(jnp.int32)
    group_index = jnp.broadcast_to(jnp.arange(G, dtype=jnp.int32)[:, None], (G, PAIR))

    def step(carry, inputs):
        diag, grad = carry
        blocks, cols, res, wrow = inputs
        wide = blocks.astype(jnp.float32)
        rounded = (wide * wrow[None, None, :, None]).astype(jnp.bfloat16)
        weighted = lax.optimization_barrier(rounded).astype(jnp.float32)
        prod = jnp.einsum('gsak,gsab->gskb', wide, weighted, precision=lax.Precision.HIGHEST)
        gterm = jnp.einsum('gsak,a->gsk', wide, wrow * res, precision=lax.Precision.HIGHEST)
        diag = diag.at[group_index, cols].add(prod)
        grad = grad.at[group_index, cols].add(gterm)
        return (diag, grad), None

    init = (jnp.zeros((G, LCB, BS, BS), jnp.float32), jnp.zeros((G, LCB, BS), jnp.float32))
    (diag, grad), unused = lax.scan(step, init, (jac_blocks, cols_by_row, residual.astype(jnp.float32), weights))
    return diag, grad
```

```python
import functools

import jax
import jax.numpy as jnp
from jax import lax
from jax.experimental import pallas as pl
from jax.experimental.pallas import tpu as pltpu
from jax.sharding import PartitionSpec as P

BS = 128
HALF = BS // 2
PAIR = 2
ROWS = BS + 8
STEPS = 32766.0
MESH = pl.DeviceIdType.MESH


def kernel(
    n_batch, n_coef, r_dev,
    jac, targets, residual, runs, scale, diag, gradient,
    items, prods, weights, firsts, seconds,
    from_twin, to_twin, packed, sides, got_packed, got_sides,
    own_sem, jac_send, jac_recv, twin_send, twin_recv, send_sem, recv_sem, side_send, side_recv,
):
    b, c = lax.axis_index("batch"), lax.axis_index("coef")
    chips = n_batch // 2
    core, chip = lax.rem(b, 2), lax.div(b, 2)
    twin = b + 1 - 2 * core
    rows = r_dev * n_coef
    n_items = rows * PAIR

    own = pltpu.make_async_copy(jac.at[:, c], items.at[c], own_sem)
    own.start()

    barrier = pltpu.get_barrier_semaphore()
    for k in range(1, n_coef):
        pl.semaphore_signal(barrier, inc=1, device_id=(b, lax.rem(c + k, n_coef)), device_id_type=MESH)
    pl.semaphore_signal(barrier, inc=1, device_id=(twin, c), device_id_type=MESH)
    for k in range(1, chips):
        pl.semaphore_signal(
            barrier, inc=1, device_id=(2 * lax.rem(chip + k, chips) + core, c), device_id_type=MESH
        )
    pl.semaphore_wait(barrier, n_coef + chips - 1)

    def jac_copy(k, r):
        peer = lax.rem(c + k, n_coef)
        return pltpu.make_async_remote_copy(
            src_ref=jac.at[r, peer], dst_ref=items.at[c, r],
            send_sem=jac_send.at[k, r], recv_sem=jac_recv.at[k, r],
            device_id=(b, peer), device_id_type=MESH,
        )

    def jac_arrival(k, r):
        source = lax.rem(c + n_coef - k, n_coef)
        return pltpu.make_async_remote_copy(
            src_ref=jac.at[r, source], dst_ref=items.at[source, r],
            send_sem=jac_send.at[k, r], recv_sem=jac_recv.at[k, r],
            device_id=(b, source), device_id_type=MESH,
        )

    for k in range(1, n_coef):
        for r in range(r_dev):
            jac_copy(k, r).start()

    n_runs = scale.shape[1]
    halves = 2 * rows
    along = jnp.broadcast_to(runs[...].astype(jnp.float32), (halves, halves))
    across = lax.broadcasted_iota(jnp.int32, (halves, halves), 0)
    beside = lax.broadcasted_iota(jnp.int32, (halves, halves), 1)
    run = jnp.sum(jnp.where(across == beside, along, 0.0), axis=1, keepdims=True).astype(jnp.int32)
    hot = lax.broadcasted_iota(jnp.int32, (halves, n_runs), 1) == run
    table = jnp.broadcast_to(scale[...].astype(jnp.float32), (halves, n_runs))
    picked = jnp.sum(jnp.where(hot, table, 0.0), axis=1, keepdims=True)
    weights[...] = jnp.broadcast_to(picked, (halves, BS))

    prods[n_items] = jnp.zeros((ROWS, BS), jnp.float32)

    def find(l, _):
        first, second = jnp.int32(n_items), jnp.int32(n_items)
        for i in range(n_items):
            hit = targets[i] == l
            second = jnp.where(hit, first, second)
            first = jnp.where(hit, i, first)
        firsts[l] = first
        seconds[l] = second
        return 0

    lax.fori_loop(0, n_batch, find, 0)

    lane = lax.broadcasted_iota(jnp.int32, (1, BS), 1)
    sub = lax.broadcasted_iota(jnp.int32, (16, BS), 0)

    def multiply(source, r):
        row = source * r_dev + r
        top = weights[pl.ds(2 * row, 1), :]
        low = weights[pl.ds(2 * row + 1, 1), :]
        scaled = jnp.where(lane < HALF, top, low) * residual[pl.ds(row, 1), :]
        part0 = scaled.astype(jnp.bfloat16).astype(jnp.float32)
        part1 = (scaled - part0).astype(jnp.bfloat16).astype(jnp.float32)
        part2 = scaled - part0 - part1
        parts = jnp.where(sub == 0, part0, jnp.where(sub == 1, part1, jnp.where(sub == 2, part2, 0.0)))
        parts = parts.astype(jnp.bfloat16)
        for s in range(PAIR):
            block = items[source, r, s]
            wide = block.astype(jnp.float32)
            weighted = jnp.concatenate([wide[:HALF] * top, wide[HALF:] * low], axis=0).astype(jnp.bfloat16)
            slot = row * PAIR + s
            prods[slot, 0:BS, :] = lax.dot_general(
                block, weighted, (((0,), (0,)), ((), ())), preferred_element_type=jnp.float32
            )
            terms = jnp.dot(parts, block, preferred_element_type=jnp.float32)
            prods[slot, BS:ROWS, :] = terms[0:8] + terms[8:16]

    own.wait()
    for r in range(r_dev):
        multiply(c, r)
    for k in range(1, n_coef):
        for r in range(r_dev):
            jac_arrival(k, r).wait_recv()
            multiply(lax.rem(c + n_coef - k, n_coef), r)

    def partial(l):
        return prods[firsts[l]] + prods[seconds[l]]

    def twin_copy(d):
        return pltpu.make_async_remote_copy(
            src_ref=to_twin.at[d], dst_ref=from_twin.at[d],
            send_sem=twin_send.at[d], recv_sem=twin_recv.at[d],
            device_id=(twin, c), device_id_type=MESH,
        )

    def to_other_core(i, _):
        d = lax.rem(i + 1, chips)
        to_twin[d] = partial(2 * lax.rem(chip + d, chips) + 1 - core)
        twin_copy(d).start()
        return 0

    lax.fori_loop(0, chips, to_other_core, 0)

    def block_copy(d):
        peer = 2 * lax.rem(chip + d, chips) + core
        return pltpu.make_async_remote_copy(
            src_ref=packed.at[d], dst_ref=got_packed.at[d],
            send_sem=send_sem.at[d], recv_sem=recv_sem.at[d],
            device_id=(peer, c), device_id_type=MESH,
        )

    def side_copy(d):
        peer = 2 * lax.rem(chip + d, chips) + core
        return pltpu.make_async_remote_copy(
            src_ref=sides.at[d], dst_ref=got_sides.at[d],
            send_sem=side_send.at[d], recv_sem=side_recv.at[d],
            device_id=(peer, c), device_id_type=MESH,
        )

    sub8 = lax.broadcasted_iota(jnp.int32, (8, BS), 0)

    def to_owner(d, _):
        mine = partial(2 * lax.rem(chip + d, chips) + core)
        twin_copy(d).wait_recv()
        total = mine + from_twin[d]
        block = total[0:BS]
        largest = jnp.maximum(jnp.max(jnp.abs(block), axis=0, keepdims=True), 2e-34)
        packed[d] = jnp.round(block * (STEPS / largest)).astype(jnp.int32).astype(jnp.int16)
        grad = jnp.sum(total[BS:ROWS], axis=0, keepdims=True)
        sides[d] = jnp.where(sub8 == 0, grad, jnp.broadcast_to(largest * (1.0 / STEPS), (8, BS)))
        block_copy(d).start()
        side_copy(d).start()
        return 0

    lax.fori_loop(1, chips, to_owner, 0)

    mine = partial(b)
    twin_copy(0).wait_recv()
    mine = mine + from_twin[0]
    diag[0, 0] = mine[0:BS]
    gradient[0] = jnp.sum(mine[BS:ROWS], axis=0, keepdims=True)

    def collect(d, _):
        side_copy(d).wait_recv()
        block_copy(d).wait_recv()
        side = got_sides[d]
        diag[0, 0] += got_packed[d].astype(jnp.int32).astype(jnp.float32) * side[1:2]
        gradient[0] += side[0:1]
        return 0

    lax.fori_loop(1, chips, collect, 0)

    for k in range(1, n_coef):
        for r in range(r_dev):
            jac_copy(k, r).wait_send()

    def finish(d, _):
        twin_copy(d).wait_send()
        return 0

    lax.fori_loop(0, chips, finish, 0)

    def finish_owner(d, _):
        side_copy(d).wait_send()
        block_copy(d).wait_send()
        return 0

    lax.fori_loop(1, chips, finish_owner, 0)


def shards(jac_blocks, col_blocks, residual, run_of_half, run_scale):
    n_batch, n_coef = lax.axis_size("batch"), lax.axis_size("coef")
    r_dev = jac_blocks.shape[0]
    rows = r_dev * n_coef
    n_items = rows * PAIR
    chips = n_batch // 2
    vmem = pl.BlockSpec(memory_space=pltpu.VMEM)
    diag, gradient = pl.pallas_call(
        functools.partial(kernel, n_batch, n_coef, r_dev),
        out_shape=(
            jax.ShapeDtypeStruct((1, 1, BS, BS), jnp.float32),
            jax.ShapeDtypeStruct((1, 1, BS), jnp.float32),
        ),
        in_specs=[
            pl.BlockSpec(memory_space=pl.ANY),
            pl.BlockSpec(memory_space=pltpu.SMEM),
            vmem, vmem, vmem,
        ],
        out_specs=(vmem, vmem),
        scratch_shapes=[
            pltpu.VMEM((n_coef, r_dev, PAIR, BS, BS), jnp.bfloat16),
            pltpu.VMEM((n_items + 1, ROWS, BS), jnp.float32),
            pltpu.VMEM((2 * rows, BS), jnp.float32),
            pltpu.SMEM((n_batch,), jnp.int32),
            pltpu.SMEM((n_batch,), jnp.int32),
            pltpu.VMEM((chips, ROWS, BS), jnp.float32),
            pltpu.VMEM((chips, ROWS, BS), jnp.float32),
            pltpu.VMEM((chips, BS, BS), jnp.int16),
            pltpu.VMEM((chips, 8, BS), jnp.float32),
            pltpu.VMEM((chips, BS, BS), jnp.int16),
            pltpu.VMEM((chips, 8, BS), jnp.float32),
            pltpu.SemaphoreType.DMA,
            pltpu.SemaphoreType.DMA((n_coef, r_dev)),
            pltpu.SemaphoreType.DMA((n_coef, r_dev)),
            pltpu.SemaphoreType.DMA((chips,)),
            pltpu.SemaphoreType.DMA((chips,)),
            pltpu.SemaphoreType.DMA((chips,)),
            pltpu.SemaphoreType.DMA((chips,)),
            pltpu.SemaphoreType.DMA((chips,)),
            pltpu.SemaphoreType.DMA((chips,)),
        ],
        compiler_params=pltpu.CompilerParams(
            collective_id=0, has_side_effects=True, vmem_limit_bytes=40 * 1024 * 1024
        ),
    )(
        jac_blocks,
        col_blocks.reshape(-1),
        residual,
        run_of_half.reshape(1, -1),
        run_scale.reshape(1, -1),
    )
    return diag, gradient


def solution(mesh):
    in_specs = (
        P(("batch", "coef"), None, None, None, None),
        P("coef", "batch", None),
        P("batch", None),
        P("batch"),
        P(),
    )
    out_specs = (P("coef", "batch", None, None), P("coef", "batch", None))
    return jax.shard_map(shards, mesh=mesh, in_specs=in_specs, out_specs=out_specs, check_vma=False)
```

```python
import functools

import jax
import jax.numpy as jnp
from jax import lax
from jax.experimental import pallas as pl
from jax.experimental.pallas import tpu as pltpu
from jax.sharding import PartitionSpec as P

BS = 128
HALF = BS // 2
PAIR = 2
ROWS = BS + 8
STEPS = 32766.0
MESH = pl.DeviceIdType.MESH


def kernel(
    n_batch, n_coef, r_dev,
    jac, targets_in, residual_in, runs_in, scale_in, result,
    items, prods, weights, firsts, seconds, targets, residual, runs, scale,
    from_twin, to_twin, packed, sides, got_packed, got_sides,
    own_sem, small_sem, jac_send, jac_recv, twin_send, twin_recv, send_sem, recv_sem, side_send, side_recv,
):
    b, c = lax.axis_index("batch"), lax.axis_index("coef")
    chips = n_batch // 2
    core, chip = lax.rem(b, 2), lax.div(b, 2)
    twin = b + 1 - 2 * core
    rows = r_dev * n_coef
    n_items = rows * PAIR

    small = [
        pltpu.make_async_copy(source, target, small_sem.at[i])
        for i, (source, target) in enumerate(
            ((runs_in, runs), (scale_in, scale), (targets_in, targets), (residual_in, residual))
        )
    ]
    for copy in small:
        copy.start()
    own = pltpu.make_async_copy(jac.at[:, c], items.at[c], own_sem)
    own.start()

    barrier = pltpu.get_barrier_semaphore()
    for k in range(1, n_coef):
        pl.semaphore_signal(barrier, inc=1, device_id=(b, lax.rem(c + k, n_coef)), device_id_type=MESH)
    pl.semaphore_signal(barrier, inc=1, device_id=(twin, c), device_id_type=MESH)
    for k in range(1, chips):
        pl.semaphore_signal(
            barrier, inc=1, device_id=(2 * lax.rem(chip + k, chips) + core, c), device_id_type=MESH
        )
    pl.semaphore_wait(barrier, n_coef + chips - 1)

    def jac_copy(k, r):
        peer = lax.rem(c + k, n_coef)
        return pltpu.make_async_remote_copy(
            src_ref=jac.at[r, peer], dst_ref=items.at[c, r],
            send_sem=jac_send.at[k, r], recv_sem=jac_recv.at[k, r],
            device_id=(b, peer), device_id_type=MESH,
        )

    def jac_arrival(k, r):
        source = lax.rem(c + n_coef - k, n_coef)
        return pltpu.make_async_remote_copy(
            src_ref=jac.at[r, source], dst_ref=items.at[source, r],
            send_sem=jac_send.at[k, r], recv_sem=jac_recv.at[k, r],
            device_id=(b, source), device_id_type=MESH,
        )

    for k in range(1, n_coef):
        for r in range(r_dev):
            jac_copy(k, r).start()

    for copy in small:
        copy.wait()
    n_runs = scale.shape[0]
    halves = 2 * rows
    along = jnp.broadcast_to(runs[...].astype(jnp.float32), (halves, halves))
    across = lax.broadcasted_iota(jnp.int32, (halves, halves), 0)
    beside = lax.broadcasted_iota(jnp.int32, (halves, halves), 1)
    run = jnp.sum(jnp.where(across == beside, along, 0.0), axis=1, keepdims=True).astype(jnp.int32)
    hot = lax.broadcasted_iota(jnp.int32, (halves, n_runs), 1) == run
    table = jnp.broadcast_to(scale[...].astype(jnp.float32).reshape(1, n_runs), (halves, n_runs))
    picked = jnp.sum(jnp.where(hot, table, 0.0), axis=1, keepdims=True)
    weights[...] = jnp.broadcast_to(picked, (halves, BS))

    prods[n_items] = jnp.zeros((ROWS, BS), jnp.float32)

    def find(l, _):
        first, second = jnp.int32(n_items), jnp.int32(n_items)
        for i in range(n_items):
            hit = targets[i % PAIR, i // PAIR] == l
            second = jnp.where(hit, first, second)
            first = jnp.where(hit, i, first)
        firsts[l] = first
        seconds[l] = second
        return 0

    lax.fori_loop(0, n_batch, find, 0)

    lane = lax.broadcasted_iota(jnp.int32, (1, BS), 1)
    sub = lax.broadcasted_iota(jnp.int32, (16, BS), 0)

    def multiply(source, r):
        row = source * r_dev + r
        top = weights[pl.ds(2 * row, 1), :]
        low = weights[pl.ds(2 * row + 1, 1), :]
        scaled = jnp.where(lane < HALF, top, low) * residual[pl.ds(row, 1), :]
        part0 = scaled.astype(jnp.bfloat16).astype(jnp.float32)
        part1 = (scaled - part0).astype(jnp.bfloat16).astype(jnp.float32)
        part2 = scaled - part0 - part1
        parts = jnp.where(sub == 0, part0, jnp.where(sub == 1, part1, jnp.where(sub == 2, part2, 0.0)))
        parts = parts.astype(jnp.bfloat16)
        for s in range(PAIR):
            block = items[source, r, s]
            wide = block.astype(jnp.float32)
            weighted = jnp.concatenate([wide[:HALF] * top, wide[HALF:] * low], axis=0).astype(jnp.bfloat16)
            slot = row * PAIR + s
            prods[slot, 0:BS, :] = lax.dot_general(
                block, weighted, (((0,), (0,)), ((), ())), preferred_element_type=jnp.float32
            )
            terms = jnp.dot(parts, block, preferred_element_type=jnp.float32)
            prods[slot, BS:ROWS, :] = terms[0:8] + terms[8:16]

    own.wait()
    for r in range(r_dev):
        multiply(c, r)
    for k in range(1, n_coef):
        for r in range(r_dev):
            jac_arrival(k, r).wait_recv()
            multiply(lax.rem(c + n_coef - k, n_coef), r)

    def partial(l):
        return prods[firsts[l]] + prods[seconds[l]]

    def twin_copy(d):
        return pltpu.make_async_remote_copy(
            src_ref=to_twin.at[d], dst_ref=from_twin.at[d],
            send_sem=twin_send.at[d], recv_sem=twin_recv.at[d],
            device_id=(twin, c), device_id_type=MESH,
        )

    def to_other_core(i, _):
        d = lax.rem(i + 1, chips)
        to_twin[d] = partial(2 * lax.rem(chip + d, chips) + 1 - core)
        twin_copy(d).start()
        return 0

    lax.fori_loop(0, chips, to_other_core, 0)

    def block_copy(d):
        peer = 2 * lax.rem(chip + d, chips) + core
        return pltpu.make_async_remote_copy(
            src_ref=packed.at[d], dst_ref=got_packed.at[d],
            send_sem=send_sem.at[d], recv_sem=recv_sem.at[d],
            device_id=(peer, c), device_id_type=MESH,
        )

    def side_copy(d):
        peer = 2 * lax.rem(chip + d, chips) + core
        return pltpu.make_async_remote_copy(
            src_ref=sides.at[d], dst_ref=got_sides.at[d],
            send_sem=side_send.at[d], recv_sem=side_recv.at[d],
            device_id=(peer, c), device_id_type=MESH,
        )

    sub8 = lax.broadcasted_iota(jnp.int32, (8, BS), 0)

    def to_owner(d, _):
        mine = partial(2 * lax.rem(chip + d, chips) + core)
        twin_copy(d).wait_recv()
        total = mine + from_twin[d]
        block = total[0:BS]
        largest = jnp.maximum(jnp.max(jnp.abs(block), axis=0, keepdims=True), 2e-34)
        packed[d] = jnp.round(block * (STEPS / largest)).astype(jnp.int32).astype(jnp.int16)
        grad = jnp.sum(total[BS:ROWS], axis=0, keepdims=True)
        sides[d] = jnp.where(sub8 == 0, grad, jnp.broadcast_to(largest * (1.0 / STEPS), (8, BS)))
        block_copy(d).start()
        side_copy(d).start()
        return 0

    lax.fori_loop(1, chips, to_owner, 0)

    mine = partial(b)
    twin_copy(0).wait_recv()
    mine = mine + from_twin[0]
    result[0:BS] = mine[0:BS]
    result[BS:ROWS] = jnp.broadcast_to(jnp.sum(mine[BS:ROWS], axis=0, keepdims=True), (8, BS))

    def collect(d, _):
        side_copy(d).wait_recv()
        block_copy(d).wait_recv()
        side = got_sides[d]
        result[0:BS] += got_packed[d].astype(jnp.int32).astype(jnp.float32) * side[1:2]
        result[BS:ROWS] += side
        return 0

    lax.fori_loop(1, chips, collect, 0)

    for k in range(1, n_coef):
        for r in range(r_dev):
            jac_copy(k, r).wait_send()

    def finish(d, _):
        twin_copy(d).wait_send()
        return 0

    lax.fori_loop(0, chips, finish, 0)

    def finish_owner(d, _):
        side_copy(d).wait_send()
        block_copy(d).wait_send()
        return 0

    lax.fori_loop(1, chips, finish_owner, 0)


def write(result, diag, gradient, sem):
    copies = (
        pltpu.make_async_copy(result.at[0:BS], diag.at[0, 0], sem.at[0]),
        pltpu.make_async_copy(result.at[BS:BS + 1], gradient.at[0], sem.at[1]),
    )
    for copy in copies:
        copy.start()
    for copy in copies:
        copy.wait()


def shards(jac_blocks, col_blocks, residual, run_of_half, run_scale):
    n_batch, n_coef = lax.axis_size("batch"), lax.axis_size("coef")
    r_dev = jac_blocks.shape[0]
    rows = r_dev * n_coef
    n_items = rows * PAIR
    chips = n_batch // 2
    vmem = pl.BlockSpec(memory_space=pltpu.VMEM)
    hbm = pl.BlockSpec(memory_space=pltpu.HBM)
    result = pl.pallas_call(
        functools.partial(kernel, n_batch, n_coef, r_dev),
        out_shape=pltpu.VMEM((ROWS, BS), jnp.float32),
        in_specs=[hbm] * 5,
        out_specs=vmem,
        scratch_shapes=[
            pltpu.VMEM((n_coef, r_dev, PAIR, BS, BS), jnp.bfloat16),
            pltpu.VMEM((n_items + 1, ROWS, BS), jnp.float32),
            pltpu.VMEM((2 * rows, BS), jnp.float32),
            pltpu.SMEM((n_batch,), jnp.int32),
            pltpu.SMEM((n_batch,), jnp.int32),
            pltpu.SMEM((PAIR, rows), jnp.int32),
            pltpu.VMEM((rows, BS), jnp.float32),
            pltpu.VMEM((1, 2 * rows), jnp.int32),
            pltpu.VMEM(run_scale.shape, run_scale.dtype),
            pltpu.VMEM((chips, ROWS, BS), jnp.float32),
            pltpu.VMEM((chips, ROWS, BS), jnp.float32),
            pltpu.VMEM((chips, BS, BS), jnp.int16),
            pltpu.VMEM((chips, 8, BS), jnp.float32),
            pltpu.VMEM((chips, BS, BS), jnp.int16),
            pltpu.VMEM((chips, 8, BS), jnp.float32),
            pltpu.SemaphoreType.DMA,
            pltpu.SemaphoreType.DMA((4,)),
            pltpu.SemaphoreType.DMA((n_coef, r_dev)),
            pltpu.SemaphoreType.DMA((n_coef, r_dev)),
            pltpu.SemaphoreType.DMA((chips,)),
            pltpu.SemaphoreType.DMA((chips,)),
            pltpu.SemaphoreType.DMA((chips,)),
            pltpu.SemaphoreType.DMA((chips,)),
            pltpu.SemaphoreType.DMA((chips,)),
            pltpu.SemaphoreType.DMA((chips,)),
        ],
        compiler_params=pltpu.CompilerParams(
            collective_id=0, has_side_effects=True, vmem_limit_bytes=60 * 1024 * 1024
        ),
    )(
        jac_blocks,
        col_blocks[0].T,
        residual,
        run_of_half.reshape(1, -1),
        run_scale,
    )
    return pl.pallas_call(
        write,
        out_shape=(
            jax.ShapeDtypeStruct((1, 1, BS, BS), jnp.float32),
            jax.ShapeDtypeStruct((1, 1, BS), jnp.float32),
        ),
        in_specs=[vmem],
        out_specs=(hbm, hbm),
        scratch_shapes=[pltpu.SemaphoreType.DMA((2,))],
    )(result)


def solution(mesh):
    in_specs = (
        P(("batch", "coef"), None, None, None, None),
        P("coef", "batch", None),
        P("batch", None),
        P("batch"),
        P(),
    )
    out_specs = (P("coef", "batch", None, None), P("coef", "batch", None))
    return jax.shard_map(shards, mesh=mesh, in_specs=in_specs, out_specs=out_specs, check_vma=False)
```

```python
import functools

import jax
import jax.numpy as jnp
from jax import lax
from jax.experimental import pallas as pl
from jax.experimental.pallas import tpu as pltpu
from jax.sharding import PartitionSpec as P

BS = 128
HALF = BS // 2
PAIR = 2
ROWS = BS + 8
STEPS = 32766.0
MESH = pl.DeviceIdType.MESH


def kernel(
    n_batch, n_coef, r_dev,
    jac, targets_in, residual_in, runs_in, scale_in, result,
    items, prods, weights, firsts, seconds, targets, residual, runs, scale,
    from_twin, to_twin, packed, sides, got_packed, got_sides,
    own_sem, small_sem, jac_send, jac_recv, twin_sem, hop_sem, side_sem,
):
    b, c = lax.axis_index("batch"), lax.axis_index("coef")
    n_line = n_batch // 4
    core, side, line = lax.rem(b, 2), lax.rem(lax.div(b, 2), 2), lax.div(b, 4)
    twin = b + 1 - 2 * core
    across_b = b + 2 - 4 * side
    turns = [(n_line // 2 + i) % n_line for i in range(n_line)]
    turns = [d for d in turns if d > 0] + [0]

    def owner(d, s, k):
        return 4 * lax.rem(line + d, n_line) + 2 * s + k

    rows = r_dev * n_coef
    n_items = rows * PAIR

    small = [
        pltpu.make_async_copy(source, target, small_sem.at[i])
        for i, (source, target) in enumerate(
            ((runs_in, runs), (scale_in, scale), (targets_in, targets), (residual_in, residual))
        )
    ]
    for copy in small:
        copy.start()
    own = pltpu.make_async_copy(jac.at[:, c], items.at[c], own_sem)
    own.start()

    barrier = pltpu.get_barrier_semaphore()
    for k in range(1, n_coef):
        pl.semaphore_signal(barrier, inc=1, device_id=(b, lax.rem(c + k, n_coef)), device_id_type=MESH)
    for peer in [twin, across_b] + [owner(d, side, core) for d in range(1, n_line)]:
        pl.semaphore_signal(barrier, inc=1, device_id=(peer, c), device_id_type=MESH)
    pl.semaphore_wait(barrier, n_coef + n_line)

    def jac_copy(k, r):
        peer = lax.rem(c + k, n_coef)
        return pltpu.make_async_remote_copy(
            src_ref=jac.at[r, peer], dst_ref=items.at[c, r],
            send_sem=jac_send.at[k, r], recv_sem=jac_recv.at[k, r],
            device_id=(b, peer), device_id_type=MESH,
        )

    def jac_arrival(k, r):
        source = lax.rem(c + n_coef - k, n_coef)
        return pltpu.make_async_remote_copy(
            src_ref=jac.at[r, source], dst_ref=items.at[source, r],
            send_sem=jac_send.at[k, r], recv_sem=jac_recv.at[k, r],
            device_id=(b, source), device_id_type=MESH,
        )

    for k in range(1, n_coef):
        for r in range(r_dev):
            jac_copy(k, r).start()

    for copy in small:
        copy.wait()
    n_runs = scale.shape[0]
    halves = 2 * rows
    along = jnp.broadcast_to(runs[...].astype(jnp.float32), (halves, halves))
    across = lax.broadcasted_iota(jnp.int32, (halves, halves), 0)
    beside = lax.broadcasted_iota(jnp.int32, (halves, halves), 1)
    run = jnp.sum(jnp.where(across == beside, along, 0.0), axis=1, keepdims=True).astype(jnp.int32)
    hot = lax.broadcasted_iota(jnp.int32, (halves, n_runs), 1) == run
    table = jnp.broadcast_to(scale[...].astype(jnp.float32).reshape(1, n_runs), (halves, n_runs))
    picked = jnp.sum(jnp.where(hot, table, 0.0), axis=1, keepdims=True)
    weights[...] = jnp.broadcast_to(picked, (halves, BS))

    prods[n_items] = jnp.zeros((ROWS, BS), jnp.float32)

    def find(l, _):
        first, second = jnp.int32(n_items), jnp.int32(n_items)
        for i in range(n_items):
            hit = targets[i % PAIR, i // PAIR] == l
            second = jnp.where(hit, first, second)
            first = jnp.where(hit, i, first)
        firsts[l] = first
        seconds[l] = second
        return 0

    lax.fori_loop(0, n_batch, find, 0)

    lane = lax.broadcasted_iota(jnp.int32, (1, BS), 1)
    sub = lax.broadcasted_iota(jnp.int32, (16, BS), 0)

    def multiply(source, r):
        row = source * r_dev + r
        top = weights[pl.ds(2 * row, 1), :]
        low = weights[pl.ds(2 * row + 1, 1), :]
        scaled = jnp.where(lane < HALF, top, low) * residual[pl.ds(row, 1), :]
        part0 = scaled.astype(jnp.bfloat16).astype(jnp.float32)
        part1 = (scaled - part0).astype(jnp.bfloat16).astype(jnp.float32)
        part2 = scaled - part0 - part1
        parts = jnp.where(sub == 0, part0, jnp.where(sub == 1, part1, jnp.where(sub == 2, part2, 0.0)))
        parts = parts.astype(jnp.bfloat16)
        for s in range(PAIR):
            block = items[source, r, s]
            wide = block.astype(jnp.float32)
            weighted = jnp.concatenate([wide[:HALF] * top, wide[HALF:] * low], axis=0).astype(jnp.bfloat16)
            slot = row * PAIR + s
            prods[slot, 0:BS, :] = lax.dot_general(
                block, weighted, (((0,), (0,)), ((), ())), preferred_element_type=jnp.float32
            )
            terms = jnp.dot(parts, block, preferred_element_type=jnp.float32)
            prods[slot, BS:ROWS, :] = terms[0:8] + terms[8:16]

    own.wait()
    for r in range(r_dev):
        multiply(c, r)
    for k in range(1, n_coef):
        for r in range(r_dev):
            jac_arrival(k, r).wait_recv()
            multiply(lax.rem(c + n_coef - k, n_coef), r)

    def partial(l):
        return prods[firsts[l]] + prods[seconds[l]]

    def send(src, dst, i, sems, peer):
        return pltpu.make_async_remote_copy(
            src_ref=src.at[i], dst_ref=dst.at[i], send_sem=sems[0].at[i], recv_sem=sems[1].at[i],
            device_id=(peer, c), device_id_type=MESH,
        )

    def twin_copy(h, d):
        return send(to_twin.at[h], from_twin.at[h], d, (twin_sem.at[0, h], twin_sem.at[1, h]), twin)

    for h in (0, 1):
        for d in turns:
            s = 1 - side if h == 0 else side
            to_twin[h, d] = partial(owner(d, s, 1 - core))
            twin_copy(h, d).start()

    sub8 = lax.broadcasted_iota(jnp.int32, (8, BS), 0)

    def hop_copies(h, d):
        peer = across_b if h == 0 else owner(d, side, core)
        return (
            send(sides.at[h], got_sides.at[h], d, (side_sem.at[0, h], side_sem.at[1, h]), peer),
            send(packed.at[h], got_packed.at[h], d, (hop_sem.at[0, h], hop_sem.at[1, h]), peer),
        )

    def pack(h, d, total):
        block = total[0:BS]
        largest = jnp.maximum(jnp.max(jnp.abs(block), axis=0, keepdims=True), 2e-34)
        packed[h, d] = jnp.round(block * (STEPS / largest)).astype(jnp.int32).astype(jnp.int16)
        grad = jnp.sum(total[BS:ROWS], axis=0, keepdims=True)
        sides[h, d] = jnp.where(sub8 == 0, grad, jnp.broadcast_to(largest * (1.0 / STEPS), (8, BS)))
        for copy in hop_copies(h, d):
            copy.start()

    def unpack(h, d):
        for copy in hop_copies(h, d):
            copy.wait_recv()
        aside = got_sides[h, d]
        block = got_packed[h, d].astype(jnp.int32).astype(jnp.float32) * aside[1:2]
        return jnp.concatenate([block, jnp.where(sub8 == 0, aside, 0.0)], axis=0)

    for d in turns:
        twin_copy(0, d).wait_recv()
        pack(0, d, partial(owner(d, 1 - side, core)) + from_twin[0, d])

    for d in turns:
        twin_copy(1, d).wait_recv()
        mine = partial(owner(d, side, core)) + from_twin[1, d]
        total = mine + unpack(0, d)
        if d > 0:
            pack(1, d, total)
    for d in turns[:-1]:
        total = total + unpack(1, d)
    result[0:BS] = total[0:BS]
    result[BS:ROWS] = jnp.broadcast_to(jnp.sum(total[BS:ROWS], axis=0, keepdims=True), (8, BS))

    for k in range(1, n_coef):
        for r in range(r_dev):
            jac_copy(k, r).wait_send()
    for h in (0, 1):
        for d in turns:
            twin_copy(h, d).wait_send()
            if h == 0 or d > 0:
                for copy in hop_copies(h, d):
                    copy.wait_send()


def write(result, diag, gradient, sem):
    copies = (
        pltpu.make_async_copy(result.at[0:BS], diag.at[0, 0], sem.at[0]),
        pltpu.make_async_copy(result.at[BS:BS + 1], gradient.at[0], sem.at[1]),
    )
    for copy in copies:
        copy.start()
    for copy in copies:
        copy.wait()


def shards(jac_blocks, col_blocks, residual, run_of_half, run_scale):
    n_batch, n_coef = lax.axis_size("batch"), lax.axis_size("coef")
    r_dev = jac_blocks.shape[0]
    rows = r_dev * n_coef
    n_items = rows * PAIR
    n_line = n_batch // 4
    vmem = pl.BlockSpec(memory_space=pltpu.VMEM)
    hbm = pl.BlockSpec(memory_space=pltpu.HBM)
    result = pl.pallas_call(
        functools.partial(kernel, n_batch, n_coef, r_dev),
        out_shape=pltpu.VMEM((ROWS, BS), jnp.float32),
        in_specs=[hbm] * 5,
        out_specs=vmem,
        scratch_shapes=[
            pltpu.VMEM((n_coef, r_dev, PAIR, BS, BS), jnp.bfloat16),
            pltpu.VMEM((n_items + 1, ROWS, BS), jnp.float32),
            pltpu.VMEM((2 * rows, BS), jnp.float32),
            pltpu.SMEM((n_batch,), jnp.int32),
            pltpu.SMEM((n_batch,), jnp.int32),
            pltpu.SMEM((PAIR, rows), jnp.int32),
            pltpu.VMEM((rows, BS), jnp.float32),
            pltpu.VMEM((1, 2 * rows), jnp.int32),
            pltpu.VMEM(run_scale.shape, run_scale.dtype),
            pltpu.VMEM((2, n_line, ROWS, BS), jnp.float32),
            pltpu.VMEM((2, n_line, ROWS, BS), jnp.float32),
            pltpu.VMEM((2, n_line, BS, BS), jnp.int16),
            pltpu.VMEM((2, n_line, 8, BS), jnp.float32),
            pltpu.VMEM((2, n_line, BS, BS), jnp.int16),
            pltpu.VMEM((2, n_line, 8, BS), jnp.float32),
            pltpu.SemaphoreType.DMA,
            pltpu.SemaphoreType.DMA((4,)),
            pltpu.SemaphoreType.DMA((n_coef, r_dev)),
            pltpu.SemaphoreType.DMA((n_coef, r_dev)),
            pltpu.SemaphoreType.DMA((2, 2, n_line)),
            pltpu.SemaphoreType.DMA((2, 2, n_line)),
            pltpu.SemaphoreType.DMA((2, 2, n_line)),
        ],
        compiler_params=pltpu.CompilerParams(
            collective_id=0, has_side_effects=True, vmem_limit_bytes=60 * 1024 * 1024
        ),
    )(
        jac_blocks,
        col_blocks[0].T,
        residual,
        run_of_half.reshape(1, -1),
        run_scale,
    )
    return pl.pallas_call(
        write,
        out_shape=(
            jax.ShapeDtypeStruct((1, 1, BS, BS), jnp.float32),
            jax.ShapeDtypeStruct((1, 1, BS), jnp.float32),
        ),
        in_specs=[vmem],
        out_specs=(hbm, hbm),
        scratch_shapes=[pltpu.SemaphoreType.DMA((2,))],
        compiler_params=pltpu.CompilerParams(vmem_limit_bytes=1024 * 1024),
    )(result)


def solution(mesh):
    in_specs = (
        P(("batch", "coef"), None, None, None, None),
        P("coef", "batch", None),
        P("batch", None),
        P("batch"),
        P(),
    )
    out_specs = (P("coef", "batch", None, None), P("coef", "batch", None))
    return jax.shard_map(shards, mesh=mesh, in_specs=in_specs, out_specs=out_specs, check_vma=False)
```

```python
import functools

import jax
import jax.numpy as jnp
from jax import lax
from jax.experimental import pallas as pl
from jax.experimental.pallas import tpu as pltpu
from jax.sharding import PartitionSpec as P

BS = 128
HALF = BS // 2
PAIR = 2
ROWS = BS + 8
STEPS = 32766.0
MESH = pl.DeviceIdType.MESH


def kernel(
    n_batch, n_coef, r_dev,
    jac, targets_in, residual_in, runs_in, scale_in, result,
    items, prods, weights, firsts, seconds, targets, residual, runs, scale,
    from_twin, to_twin, packed, sides, got_packed, got_sides,
    own_sem, small_sem, jac_send, jac_recv, twin_sem, hop_sem, side_sem,
):
    b, c = lax.axis_index("batch"), lax.axis_index("coef")
    n_line = n_batch // 4
    core, side, line = lax.rem(b, 2), lax.rem(lax.div(b, 2), 2), lax.div(b, 4)
    twin = b + 1 - 2 * core
    across_b = b + 2 - 4 * side

    def owner(t, s, k):
        return 4 * t + 2 * s + k

    others = [j + lax.div(j + n_line - line, n_line) for j in range(n_line - 1)]

    rows = r_dev * n_coef
    n_items = rows * PAIR

    small = [
        pltpu.make_async_copy(source, target, small_sem.at[i])
        for i, (source, target) in enumerate(
            ((runs_in, runs), (scale_in, scale), (targets_in, targets), (residual_in, residual))
        )
    ]
    for copy in small:
        copy.start()
    own = pltpu.make_async_copy(jac.at[:, c], items.at[c], own_sem)
    own.start()

    barrier = pltpu.get_barrier_semaphore()
    for k in range(1, n_coef):
        pl.semaphore_signal(barrier, inc=1, device_id=(b, lax.rem(c + k, n_coef)), device_id_type=MESH)
    for peer in [twin, across_b] + [owner(t, side, core) for t in others]:
        pl.semaphore_signal(barrier, inc=1, device_id=(peer, c), device_id_type=MESH)
    pl.semaphore_wait(barrier, n_coef + n_line)

    def jac_copy(k, r):
        peer = lax.rem(c + k, n_coef)
        return pltpu.make_async_remote_copy(
            src_ref=jac.at[r, peer], dst_ref=items.at[c, r],
            send_sem=jac_send.at[k, r], recv_sem=jac_recv.at[k, r],
            device_id=(b, peer), device_id_type=MESH,
        )

    def jac_arrival(k, r):
        source = lax.rem(c + n_coef - k, n_coef)
        return pltpu.make_async_remote_copy(
            src_ref=jac.at[r, source], dst_ref=items.at[source, r],
            send_sem=jac_send.at[k, r], recv_sem=jac_recv.at[k, r],
            device_id=(b, source), device_id_type=MESH,
        )

    for k in range(1, n_coef):
        for r in range(r_dev):
            jac_copy(k, r).start()

    for copy in small:
        copy.wait()
    n_runs = scale.shape[0]
    halves = 2 * rows
    along = jnp.broadcast_to(runs[...].astype(jnp.float32), (halves, halves))
    across = lax.broadcasted_iota(jnp.int32, (halves, halves), 0)
    beside = lax.broadcasted_iota(jnp.int32, (halves, halves), 1)
    run = jnp.sum(jnp.where(across == beside, along, 0.0), axis=1, keepdims=True).astype(jnp.int32)
    hot = lax.broadcasted_iota(jnp.int32, (halves, n_runs), 1) == run
    table = jnp.broadcast_to(scale[...].astype(jnp.float32).reshape(1, n_runs), (halves, n_runs))
    picked = jnp.sum(jnp.where(hot, table, 0.0), axis=1, keepdims=True)
    weights[...] = jnp.broadcast_to(picked, (halves, BS))

    prods[n_items] = jnp.zeros((ROWS, BS), jnp.float32)

    def find(l, _):
        first, second = jnp.int32(n_items), jnp.int32(n_items)
        for i in range(n_items):
            hit = targets[i % PAIR, i // PAIR] == l
            second = jnp.where(hit, first, second)
            first = jnp.where(hit, i, first)
        firsts[l] = first
        seconds[l] = second
        return 0

    lax.fori_loop(0, n_batch, find, 0)

    lane = lax.broadcasted_iota(jnp.int32, (1, BS), 1)
    sub = lax.broadcasted_iota(jnp.int32, (16, BS), 0)

    def multiply(source, r):
        row = source * r_dev + r
        top = weights[pl.ds(2 * row, 1), :]
        low = weights[pl.ds(2 * row + 1, 1), :]
        scaled = jnp.where(lane < HALF, top, low) * residual[pl.ds(row, 1), :]
        part0 = scaled.astype(jnp.bfloat16).astype(jnp.float32)
        part1 = (scaled - part0).astype(jnp.bfloat16).astype(jnp.float32)
        part2 = scaled - part0 - part1
        parts = jnp.where(sub == 0, part0, jnp.where(sub == 1, part1, jnp.where(sub == 2, part2, 0.0)))
        parts = parts.astype(jnp.bfloat16)
        both = jnp.concatenate([items[source, r, s] for s in range(PAIR)], axis=1)
        terms = jnp.dot(parts, both, preferred_element_type=jnp.float32)
        terms = terms[0:8] + terms[8:16]
        for s in range(PAIR):
            block = items[source, r, s]
            wide = block.astype(jnp.float32)
            weighted = jnp.concatenate([wide[:HALF] * top, wide[HALF:] * low], axis=0).astype(jnp.bfloat16)
            slot = row * PAIR + s
            prods[slot, 0:BS, :] = lax.dot_general(
                block, weighted, (((0,), (0,)), ((), ())), preferred_element_type=jnp.float32
            )
            prods[slot, BS:ROWS, :] = terms[:, s * BS:(s + 1) * BS]

    own.wait()
    for r in range(r_dev):
        multiply(c, r)
    for k in range(1, n_coef):
        for r in range(r_dev):
            jac_arrival(k, r).wait_recv()
            multiply(lax.rem(c + n_coef - k, n_coef), r)

    def partial(l):
        return prods[firsts[l]] + prods[seconds[l]]

    def send(src, dst, i, j, sems, peer):
        return pltpu.make_async_remote_copy(
            src_ref=src.at[i], dst_ref=dst.at[j], send_sem=sems[0].at[i], recv_sem=sems[1].at[j],
            device_id=(peer, c), device_id_type=MESH,
        )

    def twin_copy(h, d):
        return send(to_twin.at[h], from_twin.at[h], d, d, (twin_sem.at[0, h], twin_sem.at[1, h]), twin)

    for h in (0, 1):
        for t in range(n_line):
            s = 1 - side if h == 0 else side
            to_twin[h, t] = partial(owner(t, s, 1 - core))
            twin_copy(h, t).start()

    sub8 = lax.broadcasted_iota(jnp.int32, (8, BS), 0)

    def hop_copies(h, i):
        peer = across_b if h == 0 else owner(i, side, core)
        j = i if h == 0 else line
        return (
            send(sides.at[h], got_sides.at[h], i, j, (side_sem.at[0, h], side_sem.at[1, h]), peer),
            send(packed.at[h], got_packed.at[h], i, j, (hop_sem.at[0, h], hop_sem.at[1, h]), peer),
        )

    def arrivals(h, j):
        peer = across_b if h == 0 else owner(j, side, core)
        return (
            send(sides.at[h], got_sides.at[h], j, j, (side_sem.at[0, h], side_sem.at[1, h]), peer),
            send(packed.at[h], got_packed.at[h], j, j, (hop_sem.at[0, h], hop_sem.at[1, h]), peer),
        )

    def pack(h, d, total):
        block = total[0:BS]
        largest = jnp.maximum(jnp.max(jnp.abs(block), axis=0, keepdims=True), 2e-34)
        packed[h, d] = jnp.round(block * (STEPS / largest)).astype(jnp.int32).astype(jnp.int16)
        grad = jnp.sum(total[BS:ROWS], axis=0, keepdims=True)
        sides[h, d] = jnp.where(sub8 == 0, grad, jnp.broadcast_to(largest * (1.0 / STEPS), (8, BS)))
        for copy in hop_copies(h, d):
            copy.start()

    def unpack(h, d):
        for copy in arrivals(h, d):
            copy.wait_recv()
        aside = got_sides[h, d]
        block = got_packed[h, d].astype(jnp.int32).astype(jnp.float32) * aside[1:2]
        return jnp.concatenate([block, jnp.where(sub8 == 0, aside, 0.0)], axis=0)

    for t in range(n_line):
        twin_copy(0, t).wait_recv()
        pack(0, t, partial(owner(t, 1 - side, core)) + from_twin[0, t])

    for t in others + [line]:
        twin_copy(1, t).wait_recv()
        total = partial(owner(t, side, core)) + from_twin[1, t]
        total = total + unpack(0, t)
        if t is not line:
            pack(1, t, total)
    for t in others:
        total = total + unpack(1, t)
    result[0:BS] = total[0:BS]
    result[BS:ROWS] = jnp.broadcast_to(jnp.sum(total[BS:ROWS], axis=0, keepdims=True), (8, BS))

    for k in range(1, n_coef):
        for r in range(r_dev):
            jac_copy(k, r).wait_send()
    for h in (0, 1):
        for t in range(n_line):
            twin_copy(h, t).wait_send()
        for t in range(n_line) if h == 0 else others:
            for copy in hop_copies(h, t):
                copy.wait_send()


def write(result, diag, gradient, sem):
    copies = (
        pltpu.make_async_copy(result.at[0:BS], diag.at[0, 0], sem.at[0]),
        pltpu.make_async_copy(result.at[BS:BS + 1], gradient.at[0], sem.at[1]),
    )
    for copy in copies:
        copy.start()
    for copy in copies:
        copy.wait()


def shards(jac_blocks, col_blocks, residual, run_of_half, run_scale):
    n_batch, n_coef = lax.axis_size("batch"), lax.axis_size("coef")
    r_dev = jac_blocks.shape[0]
    rows = r_dev * n_coef
    n_items = rows * PAIR
    n_line = n_batch // 4
    vmem = pl.BlockSpec(memory_space=pltpu.VMEM)
    hbm = pl.BlockSpec(memory_space=pltpu.HBM)
    result = pl.pallas_call(
        functools.partial(kernel, n_batch, n_coef, r_dev),
        out_shape=pltpu.VMEM((ROWS, BS), jnp.float32),
        in_specs=[hbm] * 5,
        out_specs=vmem,
        scratch_shapes=[
            pltpu.VMEM((n_coef, r_dev, PAIR, BS, BS), jnp.bfloat16),
            pltpu.VMEM((n_items + 1, ROWS, BS), jnp.float32),
            pltpu.VMEM((2 * rows, BS), jnp.float32),
            pltpu.SMEM((n_batch,), jnp.int32),
            pltpu.SMEM((n_batch,), jnp.int32),
            pltpu.SMEM((PAIR, rows), jnp.int32),
            pltpu.VMEM((rows, BS), jnp.float32),
            pltpu.VMEM((1, 2 * rows), jnp.int32),
            pltpu.VMEM(run_scale.shape, run_scale.dtype),
            pltpu.VMEM((2, n_line, ROWS, BS), jnp.float32),
            pltpu.VMEM((2, n_line, ROWS, BS), jnp.float32),
            pltpu.VMEM((2, n_line, BS, BS), jnp.int16),
            pltpu.VMEM((2, n_line, 8, BS), jnp.float32),
            pltpu.VMEM((2, n_line, BS, BS), jnp.int16),
            pltpu.VMEM((2, n_line, 8, BS), jnp.float32),
            pltpu.SemaphoreType.DMA,
            pltpu.SemaphoreType.DMA((4,)),
            pltpu.SemaphoreType.DMA((n_coef, r_dev)),
            pltpu.SemaphoreType.DMA((n_coef, r_dev)),
            pltpu.SemaphoreType.DMA((2, 2, n_line)),
            pltpu.SemaphoreType.DMA((2, 2, n_line)),
            pltpu.SemaphoreType.DMA((2, 2, n_line)),
        ],
        compiler_params=pltpu.CompilerParams(
            collective_id=0, has_side_effects=True, vmem_limit_bytes=60 * 1024 * 1024
        ),
    )(
        jac_blocks,
        col_blocks[0].T,
        residual,
        run_of_half.reshape(1, -1),
        run_scale,
    )
    return pl.pallas_call(
        write,
        out_shape=(
            jax.ShapeDtypeStruct((1, 1, BS, BS), jnp.float32),
            jax.ShapeDtypeStruct((1, 1, BS), jnp.float32),
        ),
        in_specs=[vmem],
        out_specs=(hbm, hbm),
        scratch_shapes=[pltpu.SemaphoreType.DMA((2,))],
        compiler_params=pltpu.CompilerParams(vmem_limit_bytes=1024 * 1024),
    )(result)


def solution(mesh):
    in_specs = (
        P(("batch", "coef"), None, None, None, None),
        P("coef", "batch", None),
        P("batch", None),
        P("batch"),
        P(),
    )
    out_specs = (P("coef", "batch", None, None), P("coef", "batch", None))
    return jax.shard_map(shards, mesh=mesh, in_specs=in_specs, out_specs=out_specs, check_vma=False)
```

```python
import functools

import jax
import jax.numpy as jnp
from jax import lax
from jax.experimental import pallas as pl
from jax.experimental.pallas import tpu as pltpu
from jax.sharding import PartitionSpec as P

BS = 128
HALF = BS // 2
PAIR = 2
ROWS = BS + 8
STEPS = 32766.0
MESH = pl.DeviceIdType.MESH


def kernel(
    n_batch, n_coef, r_dev,
    jac, targets_in, residual_in, runs_in, scale_in, result,
    items, prods, weights, firsts, seconds, targets, residual, runs, scale,
    from_twin, to_twin, packed, sides, got_packed, got_sides,
    own_sem, small_sem, jac_send, jac_recv, twin_sem, hop_sem, side_sem,
):
    b, c = lax.axis_index("batch"), lax.axis_index("coef")
    chips = n_batch // 2
    core, chip = lax.rem(b, 2), lax.div(b, 2)
    twin = b + 1 - 2 * core

    others = [j + lax.div(j + chips - chip, chips) for j in range(chips - 1)]

    rows = r_dev * n_coef
    n_items = rows * PAIR

    small = [
        pltpu.make_async_copy(source, target, small_sem.at[i])
        for i, (source, target) in enumerate(
            ((runs_in, runs), (scale_in, scale), (targets_in, targets), (residual_in, residual))
        )
    ]
    for copy in small:
        copy.start()
    own = pltpu.make_async_copy(jac.at[:, c], items.at[c], own_sem)
    own.start()

    barrier = pltpu.get_barrier_semaphore()
    for k in range(1, n_coef):
        pl.semaphore_signal(barrier, inc=1, device_id=(b, lax.rem(c + k, n_coef)), device_id_type=MESH)
    for peer in [twin] + [2 * t + core for t in others]:
        pl.semaphore_signal(barrier, inc=1, device_id=(peer, c), device_id_type=MESH)
    pl.semaphore_wait(barrier, n_coef + chips - 1)

    def jac_copy(k, r):
        peer = lax.rem(c + k, n_coef)
        return pltpu.make_async_remote_copy(
            src_ref=jac.at[r, peer], dst_ref=items.at[c, r],
            send_sem=jac_send.at[k, r], recv_sem=jac_recv.at[k, r],
            device_id=(b, peer), device_id_type=MESH,
        )

    def jac_arrival(k, r):
        source = lax.rem(c + n_coef - k, n_coef)
        return pltpu.make_async_remote_copy(
            src_ref=jac.at[r, source], dst_ref=items.at[source, r],
            send_sem=jac_send.at[k, r], recv_sem=jac_recv.at[k, r],
            device_id=(b, source), device_id_type=MESH,
        )

    for k in range(1, n_coef):
        for r in range(r_dev):
            jac_copy(k, r).start()

    for copy in small:
        copy.wait()
    n_runs = scale.shape[0]
    halves = 2 * rows
    along = jnp.broadcast_to(runs[...].astype(jnp.float32), (halves, halves))
    across = lax.broadcasted_iota(jnp.int32, (halves, halves), 0)
    beside = lax.broadcasted_iota(jnp.int32, (halves, halves), 1)
    run = jnp.sum(jnp.where(across == beside, along, 0.0), axis=1, keepdims=True).astype(jnp.int32)
    hot = lax.broadcasted_iota(jnp.int32, (halves, n_runs), 1) == run
    table = jnp.broadcast_to(scale[...].astype(jnp.float32).reshape(1, n_runs), (halves, n_runs))
    picked = jnp.sum(jnp.where(hot, table, 0.0), axis=1, keepdims=True)
    weights[...] = jnp.broadcast_to(picked, (halves, BS))

    prods[n_items] = jnp.zeros((ROWS, BS), jnp.float32)

    def find(l, _):
        first, second = jnp.int32(n_items), jnp.int32(n_items)
        for i in range(n_items):
            hit = targets[i % PAIR, i // PAIR] == l
            second = jnp.where(hit, first, second)
            first = jnp.where(hit, i, first)
        firsts[l] = first
        seconds[l] = second
        return 0

    lax.fori_loop(0, n_batch, find, 0)

    lane = lax.broadcasted_iota(jnp.int32, (1, BS), 1)
    sub = lax.broadcasted_iota(jnp.int32, (16, BS), 0)

    def multiply(source, r):
        row = source * r_dev + r
        top = weights[pl.ds(2 * row, 1), :]
        low = weights[pl.ds(2 * row + 1, 1), :]
        scaled = jnp.where(lane < HALF, top, low) * residual[pl.ds(row, 1), :]
        part0 = scaled.astype(jnp.bfloat16).astype(jnp.float32)
        part1 = (scaled - part0).astype(jnp.bfloat16).astype(jnp.float32)
        part2 = scaled - part0 - part1
        parts = jnp.where(sub == 0, part0, jnp.where(sub == 1, part1, jnp.where(sub == 2, part2, 0.0)))
        parts = parts.astype(jnp.bfloat16)
        both = jnp.concatenate([items[source, r, s] for s in range(PAIR)], axis=1)
        terms = jnp.dot(parts, both, preferred_element_type=jnp.float32)
        terms = terms[0:8] + terms[8:16]
        for s in range(PAIR):
            block = items[source, r, s]
            wide = block.astype(jnp.float32)
            weighted = jnp.concatenate([wide[:HALF] * top, wide[HALF:] * low], axis=0).astype(jnp.bfloat16)
            slot = row * PAIR + s
            prods[slot, 0:BS, :] = lax.dot_general(
                block, weighted, (((0,), (0,)), ((), ())), preferred_element_type=jnp.float32
            )
            prods[slot, BS:ROWS, :] = terms[:, s * BS:(s + 1) * BS]

    own.wait()
    for r in range(r_dev):
        multiply(c, r)
    for k in range(1, n_coef):
        for r in range(r_dev):
            jac_arrival(k, r).wait_recv()
            multiply(lax.rem(c + n_coef - k, n_coef), r)

    def partial(l):
        return prods[firsts[l]] + prods[seconds[l]]

    def send(src, dst, i, j, sems, peer):
        return pltpu.make_async_remote_copy(
            src_ref=src.at[i], dst_ref=dst.at[j], send_sem=sems[0].at[i], recv_sem=sems[1].at[j],
            device_id=(peer, c), device_id_type=MESH,
        )

    def twin_copy(t):
        return send(to_twin, from_twin, t, t, (twin_sem.at[0], twin_sem.at[1]), twin)

    for t in range(chips):
        to_twin[t] = partial(2 * t + 1 - core)
        twin_copy(t).start()

    sub8 = lax.broadcasted_iota(jnp.int32, (8, BS), 0)

    def copies(i, j, peer):
        return (
            send(packed, got_packed, i, j, (hop_sem.at[0], hop_sem.at[1]), peer),
            send(sides, got_sides, i, j, (side_sem.at[0], side_sem.at[1]), peer),
        )

    for t in others:
        twin_copy(t).wait_recv()
        total = partial(2 * t + core) + from_twin[t]
        block = total[0:BS]
        largest = jnp.maximum(jnp.max(jnp.abs(block), axis=0, keepdims=True), 2e-34)
        packed[t] = jnp.round(block * (STEPS / largest)).astype(jnp.int32).astype(jnp.int16)
        grad = jnp.sum(total[BS:ROWS], axis=0, keepdims=True)
        sides[t] = jnp.where(sub8 == 0, grad, jnp.broadcast_to(largest * (1.0 / STEPS), (8, BS)))
        for copy in copies(t, chip, 2 * t + core):
            copy.start()

    twin_copy(chip).wait_recv()
    total = partial(b) + from_twin[chip]
    for t in others:
        for copy in copies(t, t, 2 * t + core):
            copy.wait_recv()
        aside = got_sides[t]
        block = got_packed[t].astype(jnp.int32).astype(jnp.float32) * aside[1:2]
        total = total + jnp.concatenate([block, jnp.where(sub8 == 0, aside, 0.0)], axis=0)
    result[0:BS] = total[0:BS]
    result[BS:ROWS] = jnp.broadcast_to(jnp.sum(total[BS:ROWS], axis=0, keepdims=True), (8, BS))

    for k in range(1, n_coef):
        for r in range(r_dev):
            jac_copy(k, r).wait_send()
    for t in range(chips):
        twin_copy(t).wait_send()
    for t in others:
        for copy in copies(t, chip, 2 * t + core):
            copy.wait_send()


def write(result, diag, gradient, sem):
    copies = (
        pltpu.make_async_copy(result.at[0:BS], diag.at[0, 0], sem.at[0]),
        pltpu.make_async_copy(result.at[BS:BS + 1], gradient.at[0], sem.at[1]),
    )
    for copy in copies:
        copy.start()
    for copy in copies:
        copy.wait()


def shards(jac_blocks, col_blocks, residual, run_of_half, run_scale):
    n_batch, n_coef = lax.axis_size("batch"), lax.axis_size("coef")
    r_dev = jac_blocks.shape[0]
    rows = r_dev * n_coef
    n_items = rows * PAIR
    chips = n_batch // 2
    vmem = pl.BlockSpec(memory_space=pltpu.VMEM)
    hbm = pl.BlockSpec(memory_space=pltpu.HBM)
    result = pl.pallas_call(
        functools.partial(kernel, n_batch, n_coef, r_dev),
        out_shape=pltpu.VMEM((ROWS, BS), jnp.float32),
        in_specs=[hbm] * 5,
        out_specs=vmem,
        scratch_shapes=[
            pltpu.VMEM((n_coef, r_dev, PAIR, BS, BS), jnp.bfloat16),
            pltpu.VMEM((n_items + 1, ROWS, BS), jnp.float32),
            pltpu.VMEM((2 * rows, BS), jnp.float32),
            pltpu.SMEM((n_batch,), jnp.int32),
            pltpu.SMEM((n_batch,), jnp.int32),
            pltpu.SMEM((PAIR, rows), jnp.int32),
            pltpu.VMEM((rows, BS), jnp.float32),
            pltpu.VMEM((1, 2 * rows), jnp.int32),
            pltpu.VMEM(run_scale.shape, run_scale.dtype),
            pltpu.VMEM((chips, ROWS, BS), jnp.float32),
            pltpu.VMEM((chips, ROWS, BS), jnp.float32),
            pltpu.VMEM((chips, BS, BS), jnp.int16),
            pltpu.VMEM((chips, 8, BS), jnp.float32),
            pltpu.VMEM((chips, BS, BS), jnp.int16),
            pltpu.VMEM((chips, 8, BS), jnp.float32),
            pltpu.SemaphoreType.DMA,
            pltpu.SemaphoreType.DMA((4,)),
            pltpu.SemaphoreType.DMA((n_coef, r_dev)),
            pltpu.SemaphoreType.DMA((n_coef, r_dev)),
            pltpu.SemaphoreType.DMA((2, chips)),
            pltpu.SemaphoreType.DMA((2, chips)),
            pltpu.SemaphoreType.DMA((2, chips)),
        ],
        compiler_params=pltpu.CompilerParams(
            collective_id=0, has_side_effects=True, vmem_limit_bytes=60 * 1024 * 1024
        ),
    )(
        jac_blocks,
        col_blocks[0].T,
        residual,
        run_of_half.reshape(1, -1),
        run_scale,
    )
    return pl.pallas_call(
        write,
        out_shape=(
            jax.ShapeDtypeStruct((1, 1, BS, BS), jnp.float32),
            jax.ShapeDtypeStruct((1, 1, BS), jnp.float32),
        ),
        in_specs=[vmem],
        out_specs=(hbm, hbm),
        scratch_shapes=[pltpu.SemaphoreType.DMA((2,))],
        compiler_params=pltpu.CompilerParams(vmem_limit_bytes=1024 * 1024),
    )(result)


def solution(mesh):
    in_specs = (
        P(("batch", "coef"), None, None, None, None),
        P("coef", "batch", None),
        P("batch", None),
        P("batch"),
        P(),
    )
    out_specs = (P("coef", "batch", None, None), P("coef", "batch", None))
    return jax.shard_map(shards, mesh=mesh, in_specs=in_specs, out_specs=out_specs, check_vma=False)
```

```python
import functools

import jax
import jax.numpy as jnp
from jax import lax
from jax.experimental import pallas as pl
from jax.experimental.pallas import tpu as pltpu
from jax.sharding import PartitionSpec as P

BS = 128
HALF = BS // 2
PAIR = 2
ROWS = BS + 8
STEPS = 32766.0
MESH = pl.DeviceIdType.MESH


def kernel(
    n_batch, n_coef, r_dev,
    jac, targets_in, residual_in, runs_in, scale_in, result,
    items, prods, weights, firsts, seconds, targets, residual, runs, scale,
    from_twin, to_twin, packed, sides, got_packed, got_sides,
    own_sem, small_sem, jac_send, jac_recv, twin_sem, hop_sem, side_sem,
):
    b, c = lax.axis_index("batch"), lax.axis_index("coef")
    chips = n_batch // 2
    n_half = chips // 4
    core, chip = lax.rem(b, 2), lax.div(b, 2)
    side, line = lax.rem(chip, 2), lax.div(chip, 2)
    twin = b + 1 - 2 * core
    half = lax.div(line, n_half)
    place = line - half * n_half
    far = [(1 - half) * n_half + j for j in range(n_half)]
    near = [half * n_half + j + lax.div(j + n_half - place, n_half) for j in range(n_half - 1)]
    here = [2 * t + side for t in near] + [2 * t + 1 - side for t in near] + [2 * line + 1 - side]
    crossing = [2 * t + side for t in far]
    crossing_pair = [2 * t + 1 - side for t in far]
    order = crossing_pair + here + crossing + [chip]

    rows = r_dev * n_coef
    n_items = rows * PAIR

    small = [
        pltpu.make_async_copy(source, target, small_sem.at[i])
        for i, (source, target) in enumerate(
            ((runs_in, runs), (scale_in, scale), (targets_in, targets), (residual_in, residual))
        )
    ]
    for copy in small:
        copy.start()
    own = pltpu.make_async_copy(jac.at[:, c], items.at[c], own_sem)
    own.start()

    barrier = pltpu.get_barrier_semaphore()
    for k in range(1, n_coef):
        pl.semaphore_signal(barrier, inc=1, device_id=(b, lax.rem(c + k, n_coef)), device_id_type=MESH)
    for peer in [twin] + [2 * t + core for t in here + crossing]:
        pl.semaphore_signal(barrier, inc=1, device_id=(peer, c), device_id_type=MESH)
    pl.semaphore_wait(barrier, n_coef + len(here) + len(crossing))

    def jac_copy(k, r):
        peer = lax.rem(c + k, n_coef)
        return pltpu.make_async_remote_copy(
            src_ref=jac.at[r, peer], dst_ref=items.at[c, r],
            send_sem=jac_send.at[k, r], recv_sem=jac_recv.at[k, r],
            device_id=(b, peer), device_id_type=MESH,
        )

    def jac_arrival(k, r):
        source = lax.rem(c + n_coef - k, n_coef)
        return pltpu.make_async_remote_copy(
            src_ref=jac.at[r, source], dst_ref=items.at[source, r],
            send_sem=jac_send.at[k, r], recv_sem=jac_recv.at[k, r],
            device_id=(b, source), device_id_type=MESH,
        )

    for k in range(1, n_coef):
        for r in range(r_dev):
            jac_copy(k, r).start()

    for copy in small:
        copy.wait()
    n_runs = scale.shape[0]
    halves = 2 * rows
    along = jnp.broadcast_to(runs[...].astype(jnp.float32), (halves, halves))
    across = lax.broadcasted_iota(jnp.int32, (halves, halves), 0)
    beside = lax.broadcasted_iota(jnp.int32, (halves, halves), 1)
    run = jnp.sum(jnp.where(across == beside, along, 0.0), axis=1, keepdims=True).astype(jnp.int32)
    hot = lax.broadcasted_iota(jnp.int32, (halves, n_runs), 1) == run
    table = jnp.broadcast_to(scale[...].astype(jnp.float32).reshape(1, n_runs), (halves, n_runs))
    picked = jnp.sum(jnp.where(hot, table, 0.0), axis=1, keepdims=True)
    weights[...] = jnp.broadcast_to(picked, (halves, BS))

    prods[n_items] = jnp.zeros((ROWS, BS), jnp.float32)

    def find(l, _):
        first, second = jnp.int32(n_items), jnp.int32(n_items)
        for i in range(n_items):
            hit = targets[i % PAIR, i // PAIR] == l
            second = jnp.where(hit, first, second)
            first = jnp.where(hit, i, first)
        firsts[l] = first
        seconds[l] = second
        return 0

    lax.fori_loop(0, n_batch, find, 0)

    lane = lax.broadcasted_iota(jnp.int32, (1, BS), 1)
    sub = lax.broadcasted_iota(jnp.int32, (16, BS), 0)

    def multiply(source, r):
        row = source * r_dev + r
        top = weights[pl.ds(2 * row, 1), :]
        low = weights[pl.ds(2 * row + 1, 1), :]
        scaled = jnp.where(lane < HALF, top, low) * residual[pl.ds(row, 1), :]
        part0 = scaled.astype(jnp.bfloat16).astype(jnp.float32)
        part1 = (scaled - part0).astype(jnp.bfloat16).astype(jnp.float32)
        part2 = scaled - part0 - part1
        parts = jnp.where(sub == 0, part0, jnp.where(sub == 1, part1, jnp.where(sub == 2, part2, 0.0)))
        parts = parts.astype(jnp.bfloat16)
        both = jnp.concatenate([items[source, r, s] for s in range(PAIR)], axis=1)
        terms = jnp.dot(parts, both, preferred_element_type=jnp.float32)
        terms = terms[0:8] + terms[8:16]
        for s in range(PAIR):
            block = items[source, r, s]
            wide = block.astype(jnp.float32)
            weighted = jnp.concatenate([wide[:HALF] * top, wide[HALF:] * low], axis=0).astype(jnp.bfloat16)
            slot = row * PAIR + s
            prods[slot, 0:BS, :] = lax.dot_general(
                block, weighted, (((0,), (0,)), ((), ())), preferred_element_type=jnp.float32
            )
            prods[slot, BS:ROWS, :] = terms[:, s * BS:(s + 1) * BS]

    own.wait()
    for r in range(r_dev):
        multiply(c, r)
    for k in range(1, n_coef):
        for r in range(r_dev):
            jac_arrival(k, r).wait_recv()
            multiply(lax.rem(c + n_coef - k, n_coef), r)

    def partial(l):
        return prods[firsts[l]] + prods[seconds[l]]

    def send(src, dst, i, j, sems, peer):
        return pltpu.make_async_remote_copy(
            src_ref=src.at[i], dst_ref=dst.at[j], send_sem=sems[0].at[i], recv_sem=sems[1].at[j],
            device_id=(peer, c), device_id_type=MESH,
        )

    def twin_copy(t):
        return send(to_twin, from_twin, t, t, (twin_sem.at[0], twin_sem.at[1]), twin)

    for t in order:
        to_twin[t] = partial(2 * t + 1 - core)
        twin_copy(t).start()

    sub8 = lax.broadcasted_iota(jnp.int32, (8, BS), 0)

    def copies(i, j, peer):
        return (
            send(packed, got_packed, i, j, (hop_sem.at[0], hop_sem.at[1]), peer),
            send(sides, got_sides, i, j, (side_sem.at[0], side_sem.at[1]), peer),
        )

    across_b = b + 2 - 4 * side

    def departures():
        hops = [copies(2 * t + 1 - side, 2 * t + side, across_b) for t in far]
        return hops + [copies(t, chip, 2 * t + core) for t in here + crossing]

    def total_of(t):
        twin_copy(t).wait_recv()
        return partial(2 * t + core) + from_twin[t]

    def pack(t, total):
        block = total[0:BS]
        largest = jnp.maximum(jnp.max(jnp.abs(block), axis=0, keepdims=True), 2e-34)
        packed[t] = jnp.round(block * (STEPS / largest)).astype(jnp.int32).astype(jnp.int16)
        grad = jnp.sum(total[BS:ROWS], axis=0, keepdims=True)
        sides[t] = jnp.where(sub8 == 0, grad, jnp.broadcast_to(largest * (1.0 / STEPS), (8, BS)))

    def unpack(t):
        for copy in copies(t, t, 2 * t + core):
            copy.wait_recv()
        aside = got_sides[t]
        block = got_packed[t].astype(jnp.int32).astype(jnp.float32) * aside[1:2]
        return jnp.concatenate([block, jnp.where(sub8 == 0, aside, 0.0)], axis=0)

    sent = departures()
    for i, t in enumerate(crossing_pair + here):
        pack(t, total_of(t))
        for copy in sent[i]:
            copy.start()
    for i, t in enumerate(crossing):
        pack(t, total_of(t) + unpack(crossing_pair[i]))
        for copy in sent[len(far) + len(here) + i]:
            copy.start()

    total = total_of(chip)
    for t in here + crossing:
        total = total + unpack(t)
    result[0:BS] = total[0:BS]
    result[BS:ROWS] = jnp.broadcast_to(jnp.sum(total[BS:ROWS], axis=0, keepdims=True), (8, BS))

    for k in range(1, n_coef):
        for r in range(r_dev):
            jac_copy(k, r).wait_send()
    for t in order:
        twin_copy(t).wait_send()
    for pair in departures():
        for copy in pair:
            copy.wait_send()


def write(result, diag, gradient, sem):
    copies = (
        pltpu.make_async_copy(result.at[0:BS], diag.at[0, 0], sem.at[0]),
        pltpu.make_async_copy(result.at[BS:BS + 1], gradient.at[0], sem.at[1]),
    )
    for copy in copies:
        copy.start()
    for copy in copies:
        copy.wait()


def shards(jac_blocks, col_blocks, residual, run_of_half, run_scale):
    n_batch, n_coef = lax.axis_size("batch"), lax.axis_size("coef")
    r_dev = jac_blocks.shape[0]
    rows = r_dev * n_coef
    n_items = rows * PAIR
    chips = n_batch // 2
    vmem = pl.BlockSpec(memory_space=pltpu.VMEM)
    hbm = pl.BlockSpec(memory_space=pltpu.HBM)
    result = pl.pallas_call(
        functools.partial(kernel, n_batch, n_coef, r_dev),
        out_shape=pltpu.VMEM((ROWS, BS), jnp.float32),
        in_specs=[hbm] * 5,
        out_specs=vmem,
        scratch_shapes=[
            pltpu.VMEM((n_coef, r_dev, PAIR, BS, BS), jnp.bfloat16),
            pltpu.VMEM((n_items + 1, ROWS, BS), jnp.float32),
            pltpu.VMEM((2 * rows, BS), jnp.float32),
            pltpu.SMEM((n_batch,), jnp.int32),
            pltpu.SMEM((n_batch,), jnp.int32),
            pltpu.SMEM((PAIR, rows), jnp.int32),
            pltpu.VMEM((rows, BS), jnp.float32),
            pltpu.VMEM((1, 2 * rows), jnp.int32),
            pltpu.VMEM(run_scale.shape, run_scale.dtype),
            pltpu.VMEM((chips, ROWS, BS), jnp.float32),
            pltpu.VMEM((chips, ROWS, BS), jnp.float32),
            pltpu.VMEM((chips, BS, BS), jnp.int16),
            pltpu.VMEM((chips, 8, BS), jnp.float32),
            pltpu.VMEM((chips, BS, BS), jnp.int16),
            pltpu.VMEM((chips, 8, BS), jnp.float32),
            pltpu.SemaphoreType.DMA,
            pltpu.SemaphoreType.DMA((4,)),
            pltpu.SemaphoreType.DMA((n_coef, r_dev)),
            pltpu.SemaphoreType.DMA((n_coef, r_dev)),
            pltpu.SemaphoreType.DMA((2, chips)),
            pltpu.SemaphoreType.DMA((2, chips)),
            pltpu.SemaphoreType.DMA((2, chips)),
        ],
        compiler_params=pltpu.CompilerParams(
            collective_id=0, has_side_effects=True, vmem_limit_bytes=60 * 1024 * 1024
        ),
    )(
        jac_blocks,
        col_blocks[0].T,
        residual,
        run_of_half.reshape(1, -1),
        run_scale,
    )
    return pl.pallas_call(
        write,
        out_shape=(
            jax.ShapeDtypeStruct((1, 1, BS, BS), jnp.float32),
            jax.ShapeDtypeStruct((1, 1, BS), jnp.float32),
        ),
        in_specs=[vmem],
        out_specs=(hbm, hbm),
        scratch_shapes=[pltpu.SemaphoreType.DMA((2,))],
        compiler_params=pltpu.CompilerParams(vmem_limit_bytes=1024 * 1024),
    )(result)


def solution(mesh):
    in_specs = (
        P(("batch", "coef"), None, None, None, None),
        P("coef", "batch", None),
        P("batch", None),
        P("batch"),
        P(),
    )
    out_specs = (P("coef", "batch", None, None), P("coef", "batch", None))
    return jax.shard_map(shards, mesh=mesh, in_specs=in_specs, out_specs=out_specs, check_vma=False)
```

```python
import functools

import jax
import jax.numpy as jnp
from jax import lax
from jax.experimental import pallas as pl
from jax.experimental.pallas import tpu as pltpu
from jax.sharding import PartitionSpec as P

BS = 128
HALF = BS // 2
PAIR = 2
ROWS = BS + 8
STEPS = 32766.0
MESH = pl.DeviceIdType.MESH


def kernel(
    n_batch, n_coef, r_dev,
    jac, targets_in, residual_in, runs_in, scale_in, result,
    items, prods, weights, firsts, seconds, targets, residual, runs, scale,
    from_twin, to_twin, packed, sides, got_packed, got_sides,
    own_sem, small_sem, jac_send, jac_recv, twin_sem, hop_sem, side_sem, line_sem,
):
    b, c = lax.axis_index("batch"), lax.axis_index("coef")
    chips = n_batch // 2
    n_half = chips // 4
    core, chip = lax.rem(b, 2), lax.div(b, 2)
    side, line = lax.rem(chip, 2), lax.div(chip, 2)
    twin = b + 1 - 2 * core
    half = lax.div(line, n_half)
    place = line - half * n_half
    far = [(1 - half) * n_half + j for j in range(n_half)]
    near = [half * n_half + j + lax.div(j + n_half - place, n_half) for j in range(n_half - 1)]
    here = [2 * t + side for t in near] + [2 * t + 1 - side for t in near] + [2 * line + 1 - side]
    crossing = [2 * t + side for t in far]
    crossing_pair = [2 * t + 1 - side for t in far]
    order = crossing_pair + here + crossing + [chip]

    rows = r_dev * n_coef
    n_items = rows * PAIR

    small = [
        pltpu.make_async_copy(source, target, small_sem.at[i])
        for i, (source, target) in enumerate(
            ((runs_in, runs), (scale_in, scale), (targets_in, targets), (residual_in, residual))
        )
    ]
    for copy in small:
        copy.start()
    own = pltpu.make_async_copy(jac.at[:, c], items.at[c], own_sem)
    own.start()

    barrier = pltpu.get_barrier_semaphore()
    n_line = chips // 2
    has_before = lax.div(line + n_line - 1, n_line)
    has_after = 1 - lax.div(line + 1, n_line)

    def tell_line(sem):
        @pl.when(has_before == 1)
        def _():
            pl.semaphore_signal(sem, inc=1, device_id=(b - 4, c), device_id_type=MESH)

        @pl.when(has_after == 1)
        def _():
            pl.semaphore_signal(sem, inc=1, device_id=(b + 4, c), device_id_type=MESH)

    for k in range(1, n_coef):
        pl.semaphore_signal(barrier, inc=1, device_id=(b, lax.rem(c + k, n_coef)), device_id_type=MESH)
    for peer in (twin, b + 2 - 4 * side):
        pl.semaphore_signal(barrier, inc=1, device_id=(peer, c), device_id_type=MESH)
    tell_line(barrier)
    pl.semaphore_wait(barrier, n_coef + 1 + has_before + has_after)

    def jac_copy(k, r):
        peer = lax.rem(c + k, n_coef)
        return pltpu.make_async_remote_copy(
            src_ref=jac.at[r, peer], dst_ref=items.at[c, r],
            send_sem=jac_send.at[k, r], recv_sem=jac_recv.at[k, r],
            device_id=(b, peer), device_id_type=MESH,
        )

    def jac_arrival(k, r):
        source = lax.rem(c + n_coef - k, n_coef)
        return pltpu.make_async_remote_copy(
            src_ref=jac.at[r, source], dst_ref=items.at[source, r],
            send_sem=jac_send.at[k, r], recv_sem=jac_recv.at[k, r],
            device_id=(b, source), device_id_type=MESH,
        )

    for k in range(1, n_coef):
        for r in range(r_dev):
            jac_copy(k, r).start()

    tell_line(line_sem.at[0])

    def next_round(k):
        pl.semaphore_wait(line_sem.at[k], has_before + has_after)
        if k + 1 < n_line - 2:
            tell_line(line_sem.at[k + 1])

    for copy in small:
        copy.wait()
    n_runs = scale.shape[0]
    halves = 2 * rows
    along = jnp.broadcast_to(runs[...].astype(jnp.float32), (halves, halves))
    across = lax.broadcasted_iota(jnp.int32, (halves, halves), 0)
    beside = lax.broadcasted_iota(jnp.int32, (halves, halves), 1)
    run = jnp.sum(jnp.where(across == beside, along, 0.0), axis=1, keepdims=True).astype(jnp.int32)
    hot = lax.broadcasted_iota(jnp.int32, (halves, n_runs), 1) == run
    table = jnp.broadcast_to(scale[...].astype(jnp.float32).reshape(1, n_runs), (halves, n_runs))
    picked = jnp.sum(jnp.where(hot, table, 0.0), axis=1, keepdims=True)
    weights[...] = jnp.broadcast_to(picked, (halves, BS))

    prods[n_items] = jnp.zeros((ROWS, BS), jnp.float32)

    def find(l, _):
        first, second = jnp.int32(n_items), jnp.int32(n_items)
        for i in range(n_items):
            hit = targets[i % PAIR, i // PAIR] == l
            second = jnp.where(hit, first, second)
            first = jnp.where(hit, i, first)
        firsts[l] = first
        seconds[l] = second
        return 0

    lax.fori_loop(0, n_batch, find, 0)

    lane = lax.broadcasted_iota(jnp.int32, (1, BS), 1)
    sub = lax.broadcasted_iota(jnp.int32, (16, BS), 0)

    def multiply(source, r):
        row = source * r_dev + r
        top = weights[pl.ds(2 * row, 1), :]
        low = weights[pl.ds(2 * row + 1, 1), :]
        scaled = jnp.where(lane < HALF, top, low) * residual[pl.ds(row, 1), :]
        part0 = scaled.astype(jnp.bfloat16).astype(jnp.float32)
        part1 = (scaled - part0).astype(jnp.bfloat16).astype(jnp.float32)
        part2 = scaled - part0 - part1
        parts = jnp.where(sub == 0, part0, jnp.where(sub == 1, part1, jnp.where(sub == 2, part2, 0.0)))
        parts = parts.astype(jnp.bfloat16)
        both = jnp.concatenate([items[source, r, s] for s in range(PAIR)], axis=1)
        terms = jnp.dot(parts, both, preferred_element_type=jnp.float32)
        terms = terms[0:8] + terms[8:16]
        for s in range(PAIR):
            block = items[source, r, s]
            wide = block.astype(jnp.float32)
            weighted = jnp.concatenate([wide[:HALF] * top, wide[HALF:] * low], axis=0).astype(jnp.bfloat16)
            slot = row * PAIR + s
            prods[slot, 0:BS, :] = lax.dot_general(
                block, weighted, (((0,), (0,)), ((), ())), preferred_element_type=jnp.float32
            )
            prods[slot, BS:ROWS, :] = terms[:, s * BS:(s + 1) * BS]

    next_round(0)
    own.wait()
    for r in range(r_dev):
        multiply(c, r)
    for k in range(1, n_line - 2):
        next_round(k)
    for k in range(1, n_coef):
        for r in range(r_dev):
            jac_arrival(k, r).wait_recv()
            multiply(lax.rem(c + n_coef - k, n_coef), r)

    def partial(l):
        return prods[firsts[l]] + prods[seconds[l]]

    def send(src, dst, i, j, sems, peer):
        return pltpu.make_async_remote_copy(
            src_ref=src.at[i], dst_ref=dst.at[j], send_sem=sems[0].at[i], recv_sem=sems[1].at[j],
            device_id=(peer, c), device_id_type=MESH,
        )

    def twin_copy(t):
        return send(to_twin, from_twin, t, t, (twin_sem.at[0], twin_sem.at[1]), twin)

    for t in order:
        to_twin[t] = partial(2 * t + 1 - core)
        twin_copy(t).start()

    sub8 = lax.broadcasted_iota(jnp.int32, (8, BS), 0)

    def copies(i, j, peer):
        return (
            send(packed, got_packed, i, j, (hop_sem.at[0], hop_sem.at[1]), peer),
            send(sides, got_sides, i, j, (side_sem.at[0], side_sem.at[1]), peer),
        )

    across_b = b + 2 - 4 * side

    def departures():
        hops = [copies(2 * t + 1 - side, 2 * t + side, across_b) for t in far]
        return hops + [copies(t, chip, 2 * t + core) for t in here + crossing]

    def total_of(t):
        twin_copy(t).wait_recv()
        return partial(2 * t + core) + from_twin[t]

    def pack(t, total):
        block = total[0:BS]
        largest = jnp.maximum(jnp.max(jnp.abs(block), axis=0, keepdims=True), 2e-34)
        packed[t] = jnp.round(block * (STEPS / largest)).astype(jnp.int32).astype(jnp.int16)
        grad = jnp.sum(total[BS:ROWS], axis=0, keepdims=True)
        sides[t] = jnp.where(sub8 == 0, grad, jnp.broadcast_to(largest * (1.0 / STEPS), (8, BS)))

    def unpack(t):
        for copy in copies(t, t, 2 * t + core):
            copy.wait_recv()
        aside = got_sides[t]
        block = got_packed[t].astype(jnp.int32).astype(jnp.float32) * aside[1:2]
        return jnp.concatenate([block, jnp.where(sub8 == 0, aside, 0.0)], axis=0)

    sent = departures()
    for i, t in enumerate(crossing_pair + here):
        pack(t, total_of(t))
        for copy in sent[i]:
            copy.start()
    for i, t in enumerate(crossing):
        pack(t, total_of(t) + unpack(crossing_pair[i]))
        for copy in sent[len(far) + len(here) + i]:
            copy.start()

    total = total_of(chip)
    for t in here + crossing:
        total = total + unpack(t)
    result[0:BS] = total[0:BS]
    result[BS:ROWS] = jnp.broadcast_to(jnp.sum(total[BS:ROWS], axis=0, keepdims=True), (8, BS))

    for k in range(1, n_coef):
        for r in range(r_dev):
            jac_copy(k, r).wait_send()
    for t in order:
        twin_copy(t).wait_send()
    for pair in departures():
        for copy in pair:
            copy.wait_send()


def write(result, diag, gradient, sem):
    copies = (
        pltpu.make_async_copy(result.at[0:BS], diag.at[0, 0], sem.at[0]),
        pltpu.make_async_copy(result.at[BS:BS + 1], gradient.at[0], sem.at[1]),
    )
    for copy in copies:
        copy.start()
    for copy in copies:
        copy.wait()


def shards(jac_blocks, col_blocks, residual, run_of_half, run_scale):
    n_batch, n_coef = lax.axis_size("batch"), lax.axis_size("coef")
    r_dev = jac_blocks.shape[0]
    rows = r_dev * n_coef
    n_items = rows * PAIR
    chips = n_batch // 2
    vmem = pl.BlockSpec(memory_space=pltpu.VMEM)
    hbm = pl.BlockSpec(memory_space=pltpu.HBM)
    result = pl.pallas_call(
        functools.partial(kernel, n_batch, n_coef, r_dev),
        out_shape=pltpu.VMEM((ROWS, BS), jnp.float32),
        in_specs=[hbm] * 5,
        out_specs=vmem,
        scratch_shapes=[
            pltpu.VMEM((n_coef, r_dev, PAIR, BS, BS), jnp.bfloat16),
            pltpu.VMEM((n_items + 1, ROWS, BS), jnp.float32),
            pltpu.VMEM((2 * rows, BS), jnp.float32),
            pltpu.SMEM((n_batch,), jnp.int32),
            pltpu.SMEM((n_batch,), jnp.int32),
            pltpu.SMEM((PAIR, rows), jnp.int32),
            pltpu.VMEM((rows, BS), jnp.float32),
            pltpu.VMEM((1, 2 * rows), jnp.int32),
            pltpu.VMEM(run_scale.shape, run_scale.dtype),
            pltpu.VMEM((chips, ROWS, BS), jnp.float32),
            pltpu.VMEM((chips, ROWS, BS), jnp.float32),
            pltpu.VMEM((chips, BS, BS), jnp.int16),
            pltpu.VMEM((chips, 8, BS), jnp.float32),
            pltpu.VMEM((chips, BS, BS), jnp.int16),
            pltpu.VMEM((chips, 8, BS), jnp.float32),
            pltpu.SemaphoreType.DMA,
            pltpu.SemaphoreType.DMA((4,)),
            pltpu.SemaphoreType.DMA((n_coef, r_dev)),
            pltpu.SemaphoreType.DMA((n_coef, r_dev)),
            pltpu.SemaphoreType.DMA((2, chips)),
            pltpu.SemaphoreType.DMA((2, chips)),
            pltpu.SemaphoreType.DMA((2, chips)),
            pltpu.SemaphoreType.REGULAR((chips // 2 - 2,)),
        ],
        compiler_params=pltpu.CompilerParams(
            collective_id=0, has_side_effects=True, vmem_limit_bytes=60 * 1024 * 1024
        ),
    )(
        jac_blocks,
        col_blocks[0].T,
        residual,
        run_of_half.reshape(1, -1),
        run_scale,
    )
    return pl.pallas_call(
        write,
        out_shape=(
            jax.ShapeDtypeStruct((1, 1, BS, BS), jnp.float32),
            jax.ShapeDtypeStruct((1, 1, BS), jnp.float32),
        ),
        in_specs=[vmem],
        out_specs=(hbm, hbm),
        scratch_shapes=[pltpu.SemaphoreType.DMA((2,))],
        compiler_params=pltpu.CompilerParams(vmem_limit_bytes=1024 * 1024),
    )(result)


def solution(mesh):
    in_specs = (
        P(("batch", "coef"), None, None, None, None),
        P("coef", "batch", None),
        P("batch", None),
        P("batch"),
        P(),
    )
    out_specs = (P("coef", "batch", None, None), P("coef", "batch", None))
    return jax.shard_map(shards, mesh=mesh, in_specs=in_specs, out_specs=out_specs, check_vma=False)
```

```python
import functools

import jax
import jax.numpy as jnp
from jax import lax
from jax.experimental import pallas as pl
from jax.experimental.pallas import tpu as pltpu
from jax.sharding import PartitionSpec as P

BS = 128
HALF = BS // 2
PAIR = 2
ROWS = BS + 8
STEPS = 32766.0
MESH = pl.DeviceIdType.MESH


def kernel(
    n_batch, n_coef, r_dev,
    jac, targets_in, residual_in, runs_in, scale_in, result,
    items, prods, weights, firsts, seconds, targets, residual, runs, scale,
    from_twin, to_twin, packed, sides, got_packed, got_sides,
    own_sem, small_sem, jac_send, jac_recv, twin_sem, hop_sem, side_sem, line_sem,
):
    b, c = lax.axis_index("batch"), lax.axis_index("coef")
    chips = n_batch // 2
    n_half = chips // 4
    core, chip = lax.rem(b, 2), lax.div(b, 2)
    side, line = lax.rem(chip, 2), lax.div(chip, 2)
    twin = b + 1 - 2 * core
    half = lax.div(line, n_half)
    place = line - half * n_half
    far = [(1 - half) * n_half + j for j in range(n_half)]
    near = [half * n_half + j + lax.div(j + n_half - place, n_half) for j in range(n_half - 1)]
    first_far = [2 * far[0] + side, 2 * far[0] + 1 - side]
    close = [2 * t + side for t in near] + [2 * t + 1 - side for t in near] + [2 * line + 1 - side]
    crossing = [2 * t + side for t in far[1:]]
    crossing_pair = [2 * t + 1 - side for t in far[1:]]
    direct = first_far + close
    order = crossing_pair + direct + crossing + [chip]

    rows = r_dev * n_coef
    n_items = rows * PAIR

    small = [
        pltpu.make_async_copy(source, target, small_sem.at[i])
        for i, (source, target) in enumerate(
            ((runs_in, runs), (scale_in, scale), (targets_in, targets), (residual_in, residual))
        )
    ]
    for copy in small:
        copy.start()
    own = pltpu.make_async_copy(jac.at[:, c], items.at[c], own_sem)
    own.start()

    barrier = pltpu.get_barrier_semaphore()
    n_line = chips // 2
    has_before = lax.div(line + n_line - 1, n_line)
    has_after = 1 - lax.div(line + 1, n_line)

    def tell_line(sem):
        @pl.when(has_before == 1)
        def _():
            pl.semaphore_signal(sem, inc=1, device_id=(b - 4, c), device_id_type=MESH)

        @pl.when(has_after == 1)
        def _():
            pl.semaphore_signal(sem, inc=1, device_id=(b + 4, c), device_id_type=MESH)

    for k in range(1, n_coef):
        pl.semaphore_signal(barrier, inc=1, device_id=(b, lax.rem(c + k, n_coef)), device_id_type=MESH)
    for peer in (twin, b + 2 - 4 * side):
        pl.semaphore_signal(barrier, inc=1, device_id=(peer, c), device_id_type=MESH)
    tell_line(barrier)
    pl.semaphore_wait(barrier, n_coef + 1 + has_before + has_after)

    def jac_copy(k, r):
        peer = lax.rem(c + k, n_coef)
        return pltpu.make_async_remote_copy(
            src_ref=jac.at[r, peer], dst_ref=items.at[c, r],
            send_sem=jac_send.at[k, r], recv_sem=jac_recv.at[k, r],
            device_id=(b, peer), device_id_type=MESH,
        )

    def jac_arrival(k, r):
        source = lax.rem(c + n_coef - k, n_coef)
        return pltpu.make_async_remote_copy(
            src_ref=jac.at[r, source], dst_ref=items.at[source, r],
            send_sem=jac_send.at[k, r], recv_sem=jac_recv.at[k, r],
            device_id=(b, source), device_id_type=MESH,
        )

    for k in range(1, n_coef):
        for r in range(r_dev):
            jac_copy(k, r).start()

    tell_line(line_sem.at[0])

    def next_round(k):
        pl.semaphore_wait(line_sem.at[k], has_before + has_after)
        if k + 1 < n_line - 1:
            tell_line(line_sem.at[k + 1])

    for copy in small:
        copy.wait()
    n_runs = scale.shape[0]
    halves = 2 * rows
    along = jnp.broadcast_to(runs[...].astype(jnp.float32), (halves, halves))
    across = lax.broadcasted_iota(jnp.int32, (halves, halves), 0)
    beside = lax.broadcasted_iota(jnp.int32, (halves, halves), 1)
    run = jnp.sum(jnp.where(across == beside, along, 0.0), axis=1, keepdims=True).astype(jnp.int32)
    hot = lax.broadcasted_iota(jnp.int32, (halves, n_runs), 1) == run
    table = jnp.broadcast_to(scale[...].astype(jnp.float32).reshape(1, n_runs), (halves, n_runs))
    picked = jnp.sum(jnp.where(hot, table, 0.0), axis=1, keepdims=True)
    weights[...] = jnp.broadcast_to(picked, (halves, BS))

    prods[n_items] = jnp.zeros((ROWS, BS), jnp.float32)

    def find(l, _):
        first, second = jnp.int32(n_items), jnp.int32(n_items)
        for i in range(n_items):
            hit = targets[i % PAIR, i // PAIR] == l
            second = jnp.where(hit, first, second)
            first = jnp.where(hit, i, first)
        firsts[l] = first
        seconds[l] = second
        return 0

    lax.fori_loop(0, n_batch, find, 0)

    lane = lax.broadcasted_iota(jnp.int32, (1, BS), 1)
    sub = lax.broadcasted_iota(jnp.int32, (16, BS), 0)

    def multiply(source, r):
        row = source * r_dev + r
        top = weights[pl.ds(2 * row, 1), :]
        low = weights[pl.ds(2 * row + 1, 1), :]
        scaled = jnp.where(lane < HALF, top, low) * residual[pl.ds(row, 1), :]
        part0 = scaled.astype(jnp.bfloat16).astype(jnp.float32)
        part1 = (scaled - part0).astype(jnp.bfloat16).astype(jnp.float32)
        part2 = scaled - part0 - part1
        parts = jnp.where(sub == 0, part0, jnp.where(sub == 1, part1, jnp.where(sub == 2, part2, 0.0)))
        parts = parts.astype(jnp.bfloat16)
        both = jnp.concatenate([items[source, r, s] for s in range(PAIR)], axis=1)
        terms = jnp.dot(parts, both, preferred_element_type=jnp.float32)
        terms = terms[0:8] + terms[8:16]
        for s in range(PAIR):
            block = items[source, r, s]
            wide = block.astype(jnp.float32)
            weighted = jnp.concatenate([wide[:HALF] * top, wide[HALF:] * low], axis=0).astype(jnp.bfloat16)
            slot = row * PAIR + s
            prods[slot, 0:BS, :] = lax.dot_general(
                block, weighted, (((0,), (0,)), ((), ())), preferred_element_type=jnp.float32
            )
            prods[slot, BS:ROWS, :] = terms[:, s * BS:(s + 1) * BS]

    next_round(0)
    own.wait()
    for r in range(r_dev):
        multiply(c, r)
    for k in range(1, n_line - 1):
        next_round(k)
    for k in range(1, n_coef):
        for r in range(r_dev):
            jac_arrival(k, r).wait_recv()
            multiply(lax.rem(c + n_coef - k, n_coef), r)

    def partial(l):
        return prods[firsts[l]] + prods[seconds[l]]

    def send(src, dst, i, j, sems, peer):
        return pltpu.make_async_remote_copy(
            src_ref=src.at[i], dst_ref=dst.at[j], send_sem=sems[0].at[i], recv_sem=sems[1].at[j],
            device_id=(peer, c), device_id_type=MESH,
        )

    def twin_copy(t):
        return send(to_twin, from_twin, t, t, (twin_sem.at[0], twin_sem.at[1]), twin)

    for t in order:
        to_twin[t] = partial(2 * t + 1 - core)
        twin_copy(t).start()

    sub8 = lax.broadcasted_iota(jnp.int32, (8, BS), 0)

    def copies(i, j, peer):
        return (
            send(packed, got_packed, i, j, (hop_sem.at[0], hop_sem.at[1]), peer),
            send(sides, got_sides, i, j, (side_sem.at[0], side_sem.at[1]), peer),
        )

    across_b = b + 2 - 4 * side

    def departures():
        hops = [copies(t, chips + i, across_b) for i, t in enumerate(crossing_pair)]
        return hops + [copies(t, chip, 2 * t + core) for t in direct + crossing]

    def total_of(t):
        twin_copy(t).wait_recv()
        return partial(2 * t + core) + from_twin[t]

    def pack(t, total):
        block = total[0:BS]
        largest = jnp.maximum(jnp.max(jnp.abs(block), axis=0, keepdims=True), 2e-34)
        packed[t] = jnp.round(block * (STEPS / largest)).astype(jnp.int32).astype(jnp.int16)
        grad = jnp.sum(total[BS:ROWS], axis=0, keepdims=True)
        sides[t] = jnp.where(sub8 == 0, grad, jnp.broadcast_to(largest * (1.0 / STEPS), (8, BS)))

    def unpack(t):
        for copy in copies(0, t, twin):
            copy.wait_recv()
        aside = got_sides[t]
        block = got_packed[t].astype(jnp.int32).astype(jnp.float32) * aside[1:2]
        return jnp.concatenate([block, jnp.where(sub8 == 0, aside, 0.0)], axis=0)

    sent = departures()
    for i, t in enumerate(crossing_pair + direct):
        pack(t, total_of(t))
        for copy in sent[i]:
            copy.start()
    for i, t in enumerate(crossing):
        pack(t, total_of(t) + unpack(chips + i))
        for copy in sent[len(crossing_pair) + len(direct) + i]:
            copy.start()

    total = total_of(chip)
    for t in close + [2 * t + side for t in far]:
        total = total + unpack(t)
    result[...] = total

    @pl.when(place == 0)
    def _():
        for t in far:
            result[...] += unpack(2 * t + 1 - side)

    result[BS:ROWS] = jnp.broadcast_to(jnp.sum(result[BS:ROWS], axis=0, keepdims=True), (8, BS))

    for k in range(1, n_coef):
        for r in range(r_dev):
            jac_copy(k, r).wait_send()
    for t in order:
        twin_copy(t).wait_send()
    for pair in departures():
        for copy in pair:
            copy.wait_send()


def write(result, diag, gradient, sem):
    copies = (
        pltpu.make_async_copy(result.at[0:BS], diag.at[0, 0], sem.at[0]),
        pltpu.make_async_copy(result.at[BS:BS + 1], gradient.at[0], sem.at[1]),
    )
    for copy in copies:
        copy.start()
    for copy in copies:
        copy.wait()


def shards(jac_blocks, col_blocks, residual, run_of_half, run_scale):
    n_batch, n_coef = lax.axis_size("batch"), lax.axis_size("coef")
    r_dev = jac_blocks.shape[0]
    rows = r_dev * n_coef
    n_items = rows * PAIR
    chips = n_batch // 2
    vmem = pl.BlockSpec(memory_space=pltpu.VMEM)
    hbm = pl.BlockSpec(memory_space=pltpu.HBM)
    result = pl.pallas_call(
        functools.partial(kernel, n_batch, n_coef, r_dev),
        out_shape=pltpu.VMEM((ROWS, BS), jnp.float32),
        in_specs=[hbm] * 5,
        out_specs=vmem,
        scratch_shapes=[
            pltpu.VMEM((n_coef, r_dev, PAIR, BS, BS), jnp.bfloat16),
            pltpu.VMEM((n_items + 1, ROWS, BS), jnp.float32),
            pltpu.VMEM((2 * rows, BS), jnp.float32),
            pltpu.SMEM((n_batch,), jnp.int32),
            pltpu.SMEM((n_batch,), jnp.int32),
            pltpu.SMEM((PAIR, rows), jnp.int32),
            pltpu.VMEM((rows, BS), jnp.float32),
            pltpu.VMEM((1, 2 * rows), jnp.int32),
            pltpu.VMEM(run_scale.shape, run_scale.dtype),
            pltpu.VMEM((chips, ROWS, BS), jnp.float32),
            pltpu.VMEM((chips, ROWS, BS), jnp.float32),
            pltpu.VMEM((chips, BS, BS), jnp.int16),
            pltpu.VMEM((chips, 8, BS), jnp.float32),
            pltpu.VMEM((chips + chips // 4, BS, BS), jnp.int16),
            pltpu.VMEM((chips + chips // 4, 8, BS), jnp.float32),
            pltpu.SemaphoreType.DMA,
            pltpu.SemaphoreType.DMA((4,)),
            pltpu.SemaphoreType.DMA((n_coef, r_dev)),
            pltpu.SemaphoreType.DMA((n_coef, r_dev)),
            pltpu.SemaphoreType.DMA((2, chips + chips // 4)),
            pltpu.SemaphoreType.DMA((2, chips + chips // 4)),
            pltpu.SemaphoreType.DMA((2, chips + chips // 4)),
            pltpu.SemaphoreType.REGULAR((chips // 2 - 1,)),
        ],
        compiler_params=pltpu.CompilerParams(
            collective_id=0, has_side_effects=True, vmem_limit_bytes=60 * 1024 * 1024
        ),
    )(
        jac_blocks,
        col_blocks[0].T,
        residual,
        run_of_half.reshape(1, -1),
        run_scale,
    )
    return pl.pallas_call(
        write,
        out_shape=(
            jax.ShapeDtypeStruct((1, 1, BS, BS), jnp.float32),
            jax.ShapeDtypeStruct((1, 1, BS), jnp.float32),
        ),
        in_specs=[vmem],
        out_specs=(hbm, hbm),
        scratch_shapes=[pltpu.SemaphoreType.DMA((2,))],
        compiler_params=pltpu.CompilerParams(vmem_limit_bytes=1024 * 1024),
    )(result)


def solution(mesh):
    in_specs = (
        P(("batch", "coef"), None, None, None, None),
        P("coef", "batch", None),
        P("batch", None),
        P("batch"),
        P(),
    )
    out_specs = (P("coef", "batch", None, None), P("coef", "batch", None))
    return jax.shard_map(shards, mesh=mesh, in_specs=in_specs, out_specs=out_specs, check_vma=False)
```

```python
import functools

import jax
import jax.numpy as jnp
from jax import lax
from jax.experimental import pallas as pl
from jax.experimental.pallas import tpu as pltpu
from jax.sharding import PartitionSpec as P

BS = 128
HALF = BS // 2
PAIR = 2
ROWS = BS + 8
STEPS = 32766.0
MESH = pl.DeviceIdType.MESH


def kernel(
    n_batch, n_coef, r_dev,
    jac, targets_in, residual_in, runs_in, scale_in, result,
    items, prods, weights, firsts, seconds, targets, residual, runs, scale,
    from_twin, to_twin, packed, sides, got_packed, got_sides,
    own_sem, small_sem, jac_send, jac_recv, twin_sem, hop_sem, side_sem, line_sem,
):
    b, c = lax.axis_index("batch"), lax.axis_index("coef")
    chips = n_batch // 2
    n_half = chips // 4
    core, chip = lax.rem(b, 2), lax.div(b, 2)
    side, line = lax.rem(chip, 2), lax.div(chip, 2)
    twin = b + 1 - 2 * core
    half = lax.div(line, n_half)
    place = line - half * n_half
    far = [(1 - half) * n_half + j for j in range(n_half)]
    near = [half * n_half + j + lax.div(j + n_half - place, n_half) for j in range(n_half - 1)]
    first_far = [2 * far[0] + side, 2 * far[0] + 1 - side]
    close = [2 * t + side for t in near] + [2 * t + 1 - side for t in near] + [2 * line + 1 - side]
    crossing = [2 * t + side for t in far[1:]]
    crossing_pair = [2 * t + 1 - side for t in far[1:]]
    direct = first_far + close
    order = first_far + crossing_pair + close + crossing + [chip]

    rows = r_dev * n_coef
    n_items = rows * PAIR

    small = [
        pltpu.make_async_copy(source, target, small_sem.at[i])
        for i, (source, target) in enumerate(
            ((runs_in, runs), (scale_in, scale), (targets_in, targets), (residual_in, residual))
        )
    ]
    for copy in small:
        copy.start()
    own = pltpu.make_async_copy(jac.at[:, c], items.at[c], own_sem)
    own.start()

    barrier = pltpu.get_barrier_semaphore()
    n_line = chips // 2
    has_before = lax.div(line + n_line - 1, n_line)
    has_after = 1 - lax.div(line + 1, n_line)

    def tell_line(sem):
        @pl.when(has_before == 1)
        def _():
            pl.semaphore_signal(sem, inc=1, device_id=(b - 4, c), device_id_type=MESH)

        @pl.when(has_after == 1)
        def _():
            pl.semaphore_signal(sem, inc=1, device_id=(b + 4, c), device_id_type=MESH)

    for k in range(1, n_coef):
        pl.semaphore_signal(barrier, inc=1, device_id=(b, lax.rem(c + k, n_coef)), device_id_type=MESH)
    for peer in (twin, b + 2 - 4 * side):
        pl.semaphore_signal(barrier, inc=1, device_id=(peer, c), device_id_type=MESH)
    tell_line(barrier)
    pl.semaphore_wait(barrier, n_coef + 1 + has_before + has_after)

    def jac_copy(k, r):
        peer = lax.rem(c + k, n_coef)
        return pltpu.make_async_remote_copy(
            src_ref=jac.at[r, peer], dst_ref=items.at[c, r],
            send_sem=jac_send.at[k, r], recv_sem=jac_recv.at[k, r],
            device_id=(b, peer), device_id_type=MESH,
        )

    def jac_arrival(k, r):
        source = lax.rem(c + n_coef - k, n_coef)
        return pltpu.make_async_remote_copy(
            src_ref=jac.at[r, source], dst_ref=items.at[source, r],
            send_sem=jac_send.at[k, r], recv_sem=jac_recv.at[k, r],
            device_id=(b, source), device_id_type=MESH,
        )

    for k in range(1, n_coef):
        for r in range(r_dev):
            jac_copy(k, r).start()

    tell_line(line_sem.at[0])

    def next_round(k):
        pl.semaphore_wait(line_sem.at[k], has_before + has_after)
        if k + 1 < n_line - 1:
            tell_line(line_sem.at[k + 1])

    for copy in small:
        copy.wait()
    n_runs = scale.shape[0]
    halves = 2 * rows
    along = jnp.broadcast_to(runs[...].astype(jnp.float32), (halves, halves))
    across = lax.broadcasted_iota(jnp.int32, (halves, halves), 0)
    beside = lax.broadcasted_iota(jnp.int32, (halves, halves), 1)
    run = jnp.sum(jnp.where(across == beside, along, 0.0), axis=1, keepdims=True).astype(jnp.int32)
    hot = lax.broadcasted_iota(jnp.int32, (halves, n_runs), 1) == run
    table = jnp.broadcast_to(scale[...].astype(jnp.float32).reshape(1, n_runs), (halves, n_runs))
    picked = jnp.sum(jnp.where(hot, table, 0.0), axis=1, keepdims=True)
    weights[...] = jnp.broadcast_to(picked, (halves, BS))

    prods[n_items] = jnp.zeros((ROWS, BS), jnp.float32)

    def find(l, _):
        first, second = jnp.int32(n_items), jnp.int32(n_items)
        for i in range(n_items):
            hit = targets[i % PAIR, i // PAIR] == l
            second = jnp.where(hit, first, second)
            first = jnp.where(hit, i, first)
        firsts[l] = first
        seconds[l] = second
        return 0

    lax.fori_loop(0, n_batch, find, 0)

    lane = lax.broadcasted_iota(jnp.int32, (1, BS), 1)
    sub = lax.broadcasted_iota(jnp.int32, (16, BS), 0)

    def multiply(source, r):
        row = source * r_dev + r
        top = weights[pl.ds(2 * row, 1), :]
        low = weights[pl.ds(2 * row + 1, 1), :]
        scaled = jnp.where(lane < HALF, top, low) * residual[pl.ds(row, 1), :]
        part0 = scaled.astype(jnp.bfloat16).astype(jnp.float32)
        part1 = (scaled - part0).astype(jnp.bfloat16).astype(jnp.float32)
        part2 = scaled - part0 - part1
        parts = jnp.where(sub == 0, part0, jnp.where(sub == 1, part1, jnp.where(sub == 2, part2, 0.0)))
        parts = parts.astype(jnp.bfloat16)
        both = jnp.concatenate([items[source, r, s] for s in range(PAIR)], axis=1)
        terms = jnp.dot(parts, both, preferred_element_type=jnp.float32)
        terms = terms[0:8] + terms[8:16]
        for s in range(PAIR):
            block = items[source, r, s]
            wide = block.astype(jnp.float32)
            weighted = jnp.concatenate([wide[:HALF] * top, wide[HALF:] * low], axis=0).astype(jnp.bfloat16)
            slot = row * PAIR + s
            prods[slot, 0:BS, :] = lax.dot_general(
                block, weighted, (((0,), (0,)), ((), ())), preferred_element_type=jnp.float32
            )
            prods[slot, BS:ROWS, :] = terms[:, s * BS:(s + 1) * BS]

    next_round(0)
    own.wait()
    for r in range(r_dev):
        multiply(c, r)
    for k in range(1, n_line - 1):
        next_round(k)
    for k in range(1, n_coef):
        for r in range(r_dev):
            jac_arrival(k, r).wait_recv()
            multiply(lax.rem(c + n_coef - k, n_coef), r)

    def partial(l):
        return prods[firsts[l]] + prods[seconds[l]]

    def send(src, dst, i, j, sems, peer):
        return pltpu.make_async_remote_copy(
            src_ref=src.at[i], dst_ref=dst.at[j], send_sem=sems[0].at[i], recv_sem=sems[1].at[j],
            device_id=(peer, c), device_id_type=MESH,
        )

    def twin_copy(t):
        return send(to_twin, from_twin, t, t, (twin_sem.at[0], twin_sem.at[1]), twin)

    for t in order:
        to_twin[t] = partial(2 * t + 1 - core)
        twin_copy(t).start()

    sub8 = lax.broadcasted_iota(jnp.int32, (8, BS), 0)

    def copies(i, j, peer):
        return (
            send(packed, got_packed, i, j, (hop_sem.at[0], hop_sem.at[1]), peer),
            send(sides, got_sides, i, j, (side_sem.at[0], side_sem.at[1]), peer),
        )

    across_b = b + 2 - 4 * side

    def departures():
        hops = [copies(t, chips + i, across_b) for i, t in enumerate(crossing_pair)]
        rest = [copies(t, chip, 2 * t + core) for t in direct + crossing]
        return rest[:2] + hops + rest[2:]

    def total_of(t):
        twin_copy(t).wait_recv()
        return partial(2 * t + core) + from_twin[t]

    def pack(t, total):
        block = total[0:BS]
        largest = jnp.maximum(jnp.max(jnp.abs(block), axis=0, keepdims=True), 2e-34)
        packed[t] = jnp.round(block * (STEPS / largest)).astype(jnp.int32).astype(jnp.int16)
        grad = jnp.sum(total[BS:ROWS], axis=0, keepdims=True)
        sides[t] = jnp.where(sub8 == 0, grad, jnp.broadcast_to(largest * (1.0 / STEPS), (8, BS)))

    def unpack(t):
        for copy in copies(0, t, twin):
            copy.wait_recv()
        aside = got_sides[t]
        block = got_packed[t].astype(jnp.int32).astype(jnp.float32) * aside[1:2]
        return jnp.concatenate([block, jnp.where(sub8 == 0, aside, 0.0)], axis=0)

    sent = departures()
    for i, t in enumerate(first_far + crossing_pair + close):
        pack(t, total_of(t))
        for copy in sent[i]:
            copy.start()
    for i, t in enumerate(crossing):
        pack(t, total_of(t) + unpack(chips + i))
        for copy in sent[len(crossing_pair) + len(direct) + i]:
            copy.start()

    total = total_of(chip)
    for t in close + [2 * t + side for t in far]:
        total = total + unpack(t)
    result[...] = total

    @pl.when(place == 0)
    def _():
        for t in far:
            result[...] += unpack(2 * t + 1 - side)

    result[BS:ROWS] = jnp.broadcast_to(jnp.sum(result[BS:ROWS], axis=0, keepdims=True), (8, BS))

    for k in range(1, n_coef):
        for r in range(r_dev):
            jac_copy(k, r).wait_send()
    for t in order:
        twin_copy(t).wait_send()
    for pair in departures():
        for copy in pair:
            copy.wait_send()


def write(result, diag, gradient, sem):
    copies = (
        pltpu.make_async_copy(result.at[0:BS], diag.at[0, 0], sem.at[0]),
        pltpu.make_async_copy(result.at[BS:BS + 1], gradient.at[0], sem.at[1]),
    )
    for copy in copies:
        copy.start()
    for copy in copies:
        copy.wait()


def shards(jac_blocks, col_blocks, residual, run_of_half, run_scale):
    n_batch, n_coef = lax.axis_size("batch"), lax.axis_size("coef")
    r_dev = jac_blocks.shape[0]
    rows = r_dev * n_coef
    n_items = rows * PAIR
    chips = n_batch // 2
    vmem = pl.BlockSpec(memory_space=pltpu.VMEM)
    hbm = pl.BlockSpec(memory_space=pltpu.HBM)
    result = pl.pallas_call(
        functools.partial(kernel, n_batch, n_coef, r_dev),
        out_shape=pltpu.VMEM((ROWS, BS), jnp.float32),
        in_specs=[hbm] * 5,
        out_specs=vmem,
        scratch_shapes=[
            pltpu.VMEM((n_coef, r_dev, PAIR, BS, BS), jnp.bfloat16),
            pltpu.VMEM((n_items + 1, ROWS, BS), jnp.float32),
            pltpu.VMEM((2 * rows, BS), jnp.float32),
            pltpu.SMEM((n_batch,), jnp.int32),
            pltpu.SMEM((n_batch,), jnp.int32),
            pltpu.SMEM((PAIR, rows), jnp.int32),
            pltpu.VMEM((rows, BS), jnp.float32),
            pltpu.VMEM((1, 2 * rows), jnp.int32),
            pltpu.VMEM(run_scale.shape, run_scale.dtype),
            pltpu.VMEM((chips, ROWS, BS), jnp.float32),
            pltpu.VMEM((chips, ROWS, BS), jnp.float32),
            pltpu.VMEM((chips, BS, BS), jnp.int16),
            pltpu.VMEM((chips, 8, BS), jnp.float32),
            pltpu.VMEM((chips + chips // 4, BS, BS), jnp.int16),
            pltpu.VMEM((chips + chips // 4, 8, BS), jnp.float32),
            pltpu.SemaphoreType.DMA,
            pltpu.SemaphoreType.DMA((4,)),
            pltpu.SemaphoreType.DMA((n_coef, r_dev)),
            pltpu.SemaphoreType.DMA((n_coef, r_dev)),
            pltpu.SemaphoreType.DMA((2, chips + chips // 4)),
            pltpu.SemaphoreType.DMA((2, chips + chips // 4)),
            pltpu.SemaphoreType.DMA((2, chips + chips // 4)),
            pltpu.SemaphoreType.REGULAR((chips // 2 - 1,)),
        ],
        compiler_params=pltpu.CompilerParams(
            collective_id=0, has_side_effects=True, vmem_limit_bytes=60 * 1024 * 1024
        ),
    )(
        jac_blocks,
        col_blocks[0].T,
        residual,
        run_of_half.reshape(1, -1),
        run_scale,
    )
    return pl.pallas_call(
        write,
        out_shape=(
            jax.ShapeDtypeStruct((1, 1, BS, BS), jnp.float32),
            jax.ShapeDtypeStruct((1, 1, BS), jnp.float32),
        ),
        in_specs=[vmem],
        out_specs=(hbm, hbm),
        scratch_shapes=[pltpu.SemaphoreType.DMA((2,))],
        compiler_params=pltpu.CompilerParams(vmem_limit_bytes=1024 * 1024),
    )(result)


def solution(mesh):
    in_specs = (
        P(("batch", "coef"), None, None, None, None),
        P("coef", "batch", None),
        P("batch", None),
        P("batch"),
        P(),
    )
    out_specs = (P("coef", "batch", None, None), P("coef", "batch", None))
    return jax.shard_map(shards, mesh=mesh, in_specs=in_specs, out_specs=out_specs, check_vma=False)
```

```python
import functools

import jax
import jax.numpy as jnp
from jax import lax
from jax.experimental import pallas as pl
from jax.experimental.pallas import tpu as pltpu
from jax.sharding import PartitionSpec as P

BS = 128
HALF = BS // 2
PAIR = 2
ROWS = BS + 8
STEPS = 32766.0
MESH = pl.DeviceIdType.MESH


def kernel(
    n_batch, n_coef, r_dev,
    jac, targets_in, residual_in, runs_in, scale_in, result,
    items, prods, weights, firsts, seconds, targets, residual, runs, scale,
    from_twin, to_twin, packed, sides, got_packed, got_sides,
    own_sem, small_sem, jac_send, jac_recv, twin_sem, hop_sem, side_sem, line_sem,
):
    b, c = lax.axis_index("batch"), lax.axis_index("coef")
    chips = n_batch // 2
    n_half = chips // 4
    core, chip = lax.rem(b, 2), lax.div(b, 2)
    side, line = lax.rem(chip, 2), lax.div(chip, 2)
    twin = b + 1 - 2 * core
    half = lax.div(line, n_half)
    place = line - half * n_half
    far = [(1 - half) * n_half + j for j in range(n_half)]
    near = [half * n_half + j + lax.div(j + n_half - place, n_half) for j in range(n_half - 1)]
    first_far = [2 * far[0] + side, 2 * far[0] + 1 - side]
    close = [2 * t + side for t in near] + [2 * t + 1 - side for t in near] + [2 * line + 1 - side]
    crossing = [2 * t + side for t in far[1:]]
    crossing_pair = [2 * t + 1 - side for t in far[1:]]
    direct = first_far + close
    order = first_far + crossing_pair + close + crossing + [chip]

    rows = r_dev * n_coef
    n_items = rows * PAIR

    small = [
        pltpu.make_async_copy(source, target, small_sem.at[i])
        for i, (source, target) in enumerate(
            ((runs_in, runs), (scale_in, scale), (targets_in, targets), (residual_in, residual))
        )
    ]
    for copy in small:
        copy.start()
    own = pltpu.make_async_copy(jac.at[:, c], items.at[c], own_sem)
    own.start()

    barrier = pltpu.get_barrier_semaphore()
    n_line = chips // 2
    has_before = lax.div(line + n_line - 1, n_line)
    has_after = 1 - lax.div(line + 1, n_line)

    def tell_line(sem):
        @pl.when(has_before == 1)
        def _():
            pl.semaphore_signal(sem, inc=1, device_id=(b - 4, c), device_id_type=MESH)

        @pl.when(has_after == 1)
        def _():
            pl.semaphore_signal(sem, inc=1, device_id=(b + 4, c), device_id_type=MESH)

    for k in range(1, n_coef):
        pl.semaphore_signal(barrier, inc=1, device_id=(b, lax.rem(c + k, n_coef)), device_id_type=MESH)
    for peer in (twin, b + 2 - 4 * side):
        pl.semaphore_signal(barrier, inc=1, device_id=(peer, c), device_id_type=MESH)
    tell_line(barrier)
    pl.semaphore_wait(barrier, n_coef + 1 + has_before + has_after)

    def jac_copy(k, r):
        peer = lax.rem(c + k, n_coef)
        return pltpu.make_async_remote_copy(
            src_ref=jac.at[r, peer], dst_ref=items.at[c, r],
            send_sem=jac_send.at[k, r], recv_sem=jac_recv.at[k, r],
            device_id=(b, peer), device_id_type=MESH,
        )

    def jac_arrival(k, r):
        source = lax.rem(c + n_coef - k, n_coef)
        return pltpu.make_async_remote_copy(
            src_ref=jac.at[r, source], dst_ref=items.at[source, r],
            send_sem=jac_send.at[k, r], recv_sem=jac_recv.at[k, r],
            device_id=(b, source), device_id_type=MESH,
        )

    for k in range(1, n_coef):
        for r in range(r_dev):
            jac_copy(k, r).start()

    tell_line(line_sem.at[0])

    def next_round(k):
        pl.semaphore_wait(line_sem.at[k], has_before + has_after)
        if k + 1 < n_line - 1:
            tell_line(line_sem.at[k + 1])

    for copy in small:
        copy.wait()
    n_runs = scale.shape[0]
    halves = 2 * rows
    along = jnp.broadcast_to(runs[...].astype(jnp.float32), (halves, halves))
    across = lax.broadcasted_iota(jnp.int32, (halves, halves), 0)
    beside = lax.broadcasted_iota(jnp.int32, (halves, halves), 1)
    run = jnp.sum(jnp.where(across == beside, along, 0.0), axis=1, keepdims=True).astype(jnp.int32)
    hot = lax.broadcasted_iota(jnp.int32, (halves, n_runs), 1) == run
    table = jnp.broadcast_to(scale[...].astype(jnp.float32).reshape(1, n_runs), (halves, n_runs))
    picked = jnp.sum(jnp.where(hot, table, 0.0), axis=1, keepdims=True)
    weights[...] = jnp.broadcast_to(picked, (halves, BS))

    prods[n_items] = jnp.zeros((ROWS, BS), jnp.float32)

    def find(l, _):
        first, second = jnp.int32(n_items), jnp.int32(n_items)
        for i in range(n_items):
            hit = targets[i % PAIR, i // PAIR] == l
            second = jnp.where(hit, first, second)
            first = jnp.where(hit, i, first)
        firsts[l] = first
        seconds[l] = second
        return 0

    lax.fori_loop(0, n_batch, find, 0)

    lane = lax.broadcasted_iota(jnp.int32, (1, BS), 1)
    sub = lax.broadcasted_iota(jnp.int32, (16, BS), 0)

    def multiply(source, r):
        row = source * r_dev + r
        top = weights[pl.ds(2 * row, 1), :]
        low = weights[pl.ds(2 * row + 1, 1), :]
        scaled = jnp.where(lane < HALF, top, low) * residual[pl.ds(row, 1), :]
        part0 = scaled.astype(jnp.bfloat16).astype(jnp.float32)
        part1 = (scaled - part0).astype(jnp.bfloat16).astype(jnp.float32)
        part2 = scaled - part0 - part1
        parts = jnp.where(sub == 0, part0, jnp.where(sub == 1, part1, jnp.where(sub == 2, part2, 0.0)))
        parts = parts.astype(jnp.bfloat16)
        both = jnp.concatenate([items[source, r, s] for s in range(PAIR)], axis=1)
        terms = jnp.dot(parts, both, preferred_element_type=jnp.float32)
        terms = terms[0:8] + terms[8:16]
        for s in range(PAIR):
            block = items[source, r, s]
            wide = block.astype(jnp.float32)
            weighted = jnp.concatenate([wide[:HALF] * top, wide[HALF:] * low], axis=0).astype(jnp.bfloat16)
            slot = row * PAIR + s
            prods[slot, 0:BS, :] = lax.dot_general(
                block, weighted, (((0,), (0,)), ((), ())), preferred_element_type=jnp.float32
            )
            prods[slot, BS:ROWS, :] = terms[:, s * BS:(s + 1) * BS]

    own.wait()
    rounds = list(range(n_line - 1))
    for r in range(r_dev):
        multiply(c, r)
        if r % 2 == 0 and rounds:
            next_round(rounds.pop(0))
    for k in range(1, n_coef):
        for r in range(r_dev):
            jac_arrival(k, r).wait_recv()
            multiply(lax.rem(c + n_coef - k, n_coef), r)
            if rounds:
                next_round(rounds.pop(0))
    for k in rounds:
        next_round(k)

    def partial(l):
        return prods[firsts[l]] + prods[seconds[l]]

    def send(src, dst, i, j, sems, peer):
        return pltpu.make_async_remote_copy(
            src_ref=src.at[i], dst_ref=dst.at[j], send_sem=sems[0].at[i], recv_sem=sems[1].at[j],
            device_id=(peer, c), device_id_type=MESH,
        )

    def twin_copy(t):
        return send(to_twin, from_twin, t, t, (twin_sem.at[0], twin_sem.at[1]), twin)

    for t in order:
        to_twin[t] = partial(2 * t + 1 - core)
        twin_copy(t).start()

    sub8 = lax.broadcasted_iota(jnp.int32, (8, BS), 0)

    def copies(i, j, peer):
        return (
            send(packed, got_packed, i, j, (hop_sem.at[0], hop_sem.at[1]), peer),
            send(sides, got_sides, i, j, (side_sem.at[0], side_sem.at[1]), peer),
        )

    across_b = b + 2 - 4 * side

    def departures():
        hops = [copies(t, chips + i, across_b) for i, t in enumerate(crossing_pair)]
        rest = [copies(t, chip, 2 * t + core) for t in direct + crossing]
        return rest[:2] + hops + rest[2:]

    def total_of(t):
        twin_copy(t).wait_recv()
        return partial(2 * t + core) + from_twin[t]

    def pack(t, total):
        block = total[0:BS]
        largest = jnp.maximum(jnp.max(jnp.abs(block), axis=0, keepdims=True), 2e-34)
        packed[t] = jnp.round(block * (STEPS / largest)).astype(jnp.int32).astype(jnp.int16)
        grad = jnp.sum(total[BS:ROWS], axis=0, keepdims=True)
        sides[t] = jnp.where(sub8 == 0, grad, jnp.broadcast_to(largest * (1.0 / STEPS), (8, BS)))

    def unpack(t):
        for copy in copies(0, t, twin):
            copy.wait_recv()
        aside = got_sides[t]
        block = got_packed[t].astype(jnp.int32).astype(jnp.float32) * aside[1:2]
        return jnp.concatenate([block, jnp.where(sub8 == 0, aside, 0.0)], axis=0)

    sent = departures()
    for i, t in enumerate(first_far + crossing_pair + close):
        pack(t, total_of(t))
        for copy in sent[i]:
            copy.start()
    for i, t in enumerate(crossing):
        pack(t, total_of(t) + unpack(chips + i))
        for copy in sent[len(crossing_pair) + len(direct) + i]:
            copy.start()

    total = total_of(chip)
    for t in close + [2 * t + side for t in far]:
        total = total + unpack(t)
    result[...] = total

    @pl.when(place == 0)
    def _():
        for t in far:
            result[...] += unpack(2 * t + 1 - side)

    result[BS:ROWS] = jnp.broadcast_to(jnp.sum(result[BS:ROWS], axis=0, keepdims=True), (8, BS))

    for k in range(1, n_coef):
        for r in range(r_dev):
            jac_copy(k, r).wait_send()
    for t in order:
        twin_copy(t).wait_send()
    for pair in departures():
        for copy in pair:
            copy.wait_send()


def write(result, diag, gradient, sem):
    copies = (
        pltpu.make_async_copy(result.at[0:BS], diag.at[0, 0], sem.at[0]),
        pltpu.make_async_copy(result.at[BS:BS + 1], gradient.at[0], sem.at[1]),
    )
    for copy in copies:
        copy.start()
    for copy in copies:
        copy.wait()


def shards(jac_blocks, col_blocks, residual, run_of_half, run_scale):
    n_batch, n_coef = lax.axis_size("batch"), lax.axis_size("coef")
    r_dev = jac_blocks.shape[0]
    rows = r_dev * n_coef
    n_items = rows * PAIR
    chips = n_batch // 2
    vmem = pl.BlockSpec(memory_space=pltpu.VMEM)
    hbm = pl.BlockSpec(memory_space=pltpu.HBM)
    result = pl.pallas_call(
        functools.partial(kernel, n_batch, n_coef, r_dev),
        out_shape=pltpu.VMEM((ROWS, BS), jnp.float32),
        in_specs=[hbm] * 5,
        out_specs=vmem,
        scratch_shapes=[
            pltpu.VMEM((n_coef, r_dev, PAIR, BS, BS), jnp.bfloat16),
            pltpu.VMEM((n_items + 1, ROWS, BS), jnp.float32),
            pltpu.VMEM((2 * rows, BS), jnp.float32),
            pltpu.SMEM((n_batch,), jnp.int32),
            pltpu.SMEM((n_batch,), jnp.int32),
            pltpu.SMEM((PAIR, rows), jnp.int32),
            pltpu.VMEM((rows, BS), jnp.float32),
            pltpu.VMEM((1, 2 * rows), jnp.int32),
            pltpu.VMEM(run_scale.shape, run_scale.dtype),
            pltpu.VMEM((chips, ROWS, BS), jnp.float32),
            pltpu.VMEM((chips, ROWS, BS), jnp.float32),
            pltpu.VMEM((chips, BS, BS), jnp.int16),
            pltpu.VMEM((chips, 8, BS), jnp.float32),
            pltpu.VMEM((chips + chips // 4, BS, BS), jnp.int16),
            pltpu.VMEM((chips + chips // 4, 8, BS), jnp.float32),
            pltpu.SemaphoreType.DMA,
            pltpu.SemaphoreType.DMA((4,)),
            pltpu.SemaphoreType.DMA((n_coef, r_dev)),
            pltpu.SemaphoreType.DMA((n_coef, r_dev)),
            pltpu.SemaphoreType.DMA((2, chips + chips // 4)),
            pltpu.SemaphoreType.DMA((2, chips + chips // 4)),
            pltpu.SemaphoreType.DMA((2, chips + chips // 4)),
            pltpu.SemaphoreType.REGULAR((chips // 2 - 1,)),
        ],
        compiler_params=pltpu.CompilerParams(
            collective_id=0, has_side_effects=True, vmem_limit_bytes=60 * 1024 * 1024
        ),
    )(
        jac_blocks,
        col_blocks[0].T,
        residual,
        run_of_half.reshape(1, -1),
        run_scale,
    )
    return pl.pallas_call(
        write,
        out_shape=(
            jax.ShapeDtypeStruct((1, 1, BS, BS), jnp.float32),
            jax.ShapeDtypeStruct((1, 1, BS), jnp.float32),
        ),
        in_specs=[vmem],
        out_specs=(hbm, hbm),
        scratch_shapes=[pltpu.SemaphoreType.DMA((2,))],
        compiler_params=pltpu.CompilerParams(vmem_limit_bytes=1024 * 1024),
    )(result)


def solution(mesh):
    in_specs = (
        P(("batch", "coef"), None, None, None, None),
        P("coef", "batch", None),
        P("batch", None),
        P("batch"),
        P(),
    )
    out_specs = (P("coef", "batch", None, None), P("coef", "batch", None))
    return jax.shard_map(shards, mesh=mesh, in_specs=in_specs, out_specs=out_specs, check_vma=False)
```
